256 devices in a mesh: pos: 8 (over y_hi, x), beam: 32 (over z, y_lo, core).
Axes of the slice: x: 4, y: 4 (y_hi: 2, y_lo: 2; y = y_hi * 2 + y_lo), z: 8, core: 2. Of those that a mesh axis runs over, the one named last changes fastest.
Arguments:
- s_matrix: bfloat16 [2048, 2, 144, 256], P('beam'), may hold values from -0.119628906 to 0.119628906
- beam_index: int32 [2048, 2], P('beam'), may hold values from -24 to 24
- amplitude: float32 [2048], P('beam'), may hold values from 0.3 to 3
- phase: float32 [2048], P('beam'), may hold values from -3.140625 to 3.140625
- offsets_y: int32 [32], replicated, may hold values from 0 to 16
- offsets_x: int32 [32], replicated, may hold values from 0 to 128
- measured: float32 [32, 128, 128], P('pos'), may hold values from 0.3 to 2
Outputs:
- s_gradient: float32 [2048, 2, 144, 256], P('beam', None, 'pos')
The draws below stay inside these ranges and needn't reach their ends.
All inputs are finite; a program needn't handle non-finite values.
Results may differ from the reference program's by a relative error of at most 0.007.
Values sent between devices are 32-bit elements; how exact they have to be, the bound alone decides.
No kernel may reach another device: no remote copies, remote signals or barrier semaphores. Data moves between devices by JAX's collectives and lax.ppermute only.
A program may use at most 128 MiB of HBM per device.

```python
import math
import jax
import jax.numpy as jnp
from jax import lax

BEAMS = 2048
WIN = 128
FIELD_Y = 144
FIELD_X = 256
POSITIONS = 32


def place_ends(result, own_key, low, top_value):
    place = [jax.random.randint(jax.random.fold_in(own_key, axis), (), 0, length) for axis, length in enumerate(result.shape)]
    main_axis = result.shape.index(max(result.shape))
    neighbour = place[:main_axis] + [(place[main_axis] + 1) % result.shape[main_axis]] + place[main_axis + 1:]
    return result.at[tuple(place)].set(low).at[tuple(neighbour)].set(top_value)


def shard_levels(own_key, dims, cuts, least, largest):
    def one(axis_at, shards_of):
        steps = jax.random.uniform(jax.random.fold_in(jax.random.fold_in(own_key, 6), axis_at), (shards_of,), jnp.float32, least / len(cuts), largest / len(cuts))
        return jnp.repeat(jnp.exp(steps), dims[axis_at] // shards_of).reshape((-1,) + (1,) * (len(dims) - axis_at - 1))

    factor_of = one(*cuts[0])
    for cut in cuts[1:]:
        factor_of = factor_of * one(*cut)
    return factor_of


def gaussian(stream_key, extent, deviation, bound, split=(), kind=jnp.bfloat16):
    result = jax.random.normal(stream_key, extent, jnp.float32) * deviation
    if len(split) > 0:
        result = shard_levels(stream_key, extent, split, -0.22, 0.18) * result
    return jnp.clip(result, min=-bound, max=bound).astype(kind)


def setup_inputs(seed: int = 0) -> dict:
    keys = jax.random.split(jax.random.key(seed), 8)
    return {
        "s_matrix": gaussian(keys[0], (BEAMS, 2, FIELD_Y, FIELD_X), 0.015, 0.119628906, ((0, 32),)),
        "beam_index": place_ends(jax.random.randint(keys[1], (BEAMS, 2), -24, 25), jax.random.fold_in(keys[1], 1), -24, 24).astype(jnp.int32),
        "amplitude": jnp.clip(jnp.exp(math.log(3.0) - 2.3025851 * jax.random.uniform(keys[2], (BEAMS,), jnp.float32) ** shard_levels(keys[2], (BEAMS,), ((0, 32),), -0.2, 0.2)), 0.3, 3.0),
        "phase": jnp.clip(jax.random.uniform(keys[3], (BEAMS,), jnp.float32, -3.140625, 3.140625), -3.140625, 3.140625),
        "offsets_y": place_ends(jax.random.randint(keys[4], (POSITIONS,), 0, FIELD_Y - WIN + 1), jax.random.fold_in(keys[4], 1), 0, FIELD_Y - WIN).astype(jnp.int32),
        "offsets_x": place_ends(jax.random.randint(keys[5], (POSITIONS,), 0, FIELD_X - WIN + 1), jax.random.fold_in(keys[5], 1), 0, FIELD_X - WIN).astype(jnp.int32),
        "measured": jnp.clip(0.3 + 1.7 * jax.random.uniform(keys[6], (POSITIONS, WIN, WIN), jnp.float32) ** shard_levels(keys[6], (POSITIONS, WIN, WIN), ((0, 8),), -0.2, 0.2), 0.3, 2.0),
    }


def beam_weights(rows_y, cols_x, beam_index, amplitude, phase):
    wave_y = beam_index[:, 0]
    wave_x = beam_index[:, 1]
    turns = jnp.mod(rows_y[:, None] * wave_y[None, :] * FIELD_X + cols_x[:, None] * wave_x[None, :] * FIELD_Y, FIELD_Y * FIELD_X)
    angles = phase[None, :] - (2.0 * math.pi / (FIELD_Y * FIELD_X)) * turns.astype(jnp.float32)
    real_coef = (amplitude[None, :] * jnp.cos(angles)).astype(jnp.bfloat16)
    imag_coef = (amplitude[None, :] * jnp.sin(angles)).astype(jnp.bfloat16)
    return real_coef, imag_coef


def mixing(real_coef, imag_coef):
    upper = jnp.stack([real_coef, -imag_coef], axis=-1).reshape(-1)
    lower = jnp.stack([imag_coef, real_coef], axis=-1).reshape(-1)
    return jnp.stack([upper, lower])


def exit_wave(s_matrix, row_y, col_x, real_coef, imag_coef):
    beams_here = s_matrix.shape[0]
    anchor = jnp.zeros((), jnp.int32)
    window = lax.dynamic_slice(s_matrix, (anchor, anchor, row_y, col_x), (beams_here, 2, WIN, WIN))
    window = window.reshape(beams_here * 2, WIN * WIN)
    return jnp.dot(mixing(real_coef, imag_coef), window, preferred_element_type=jnp.float32).reshape(2, WIN, WIN)


def gradient_matrix(real_coef, imag_coef):
    real_wide = real_coef.astype(jnp.float32).T
    imag_wide = imag_coef.astype(jnp.float32).T
    upper = jnp.stack([real_wide, imag_wide], axis=-1)
    lower = jnp.stack([-imag_wide, real_wide], axis=-1)
    return jnp.stack([upper, lower], axis=1).reshape(real_wide.shape[0] * 2, -1)


def place_full(plane, row_y, col_x):
    frame = jnp.zeros((2, FIELD_Y, FIELD_X), jnp.float32)
    return lax.dynamic_update_slice(frame, plane, (jnp.zeros((), jnp.int32), row_y, col_x))


def reference(s_matrix, beam_index, amplitude, phase, offsets_y, offsets_x, measured):
    real_coef, imag_coef = beam_weights(offsets_y, offsets_x, beam_index, amplitude, phase)
    waves = lax.map(lambda items: exit_wave(s_matrix, items[0], items[1], items[2], items[3]), (offsets_y, offsets_x, real_coef, imag_coef))
    far = jnp.fft.fft2(waves[:, 0] + 1j * waves[:, 1], norm="ortho")
    factor = 1.0 - measured / jnp.maximum(jnp.abs(far), 0.5)
    back = jnp.fft.ifft2(far * factor, norm="ortho")
    planes = jnp.stack([jnp.real(back), jnp.imag(back)], axis=1).astype(jnp.float32)
    placed = jax.vmap(place_full)(planes, offsets_y, offsets_x)
    weights = gradient_matrix(real_coef, imag_coef)
    total = jnp.dot(weights, placed.reshape(POSITIONS * 2, FIELD_Y * FIELD_X), precision=lax.Precision.HIGHEST)
    return total.reshape(BEAMS, 2, FIELD_Y, FIELD_X).astype(jnp.float32)
```

```python
import math

import jax
import jax.numpy as jnp
import numpy as np
from jax import lax
from jax.experimental import pallas as pl
from jax.experimental.pallas import tpu as pltpu
from jax.sharding import Mesh
from jax.sharding import PartitionSpec as P

WIN = 128
FIELD_Y = 144
FIELD_X = 256
BANDS = 8
BAND = FIELD_Y // BANDS
BLOCK = 40
ROWS = 16
LIMIT = 48 * 1024 * 1024


def beam_weights(rows_y, cols_x, beam_index, amplitude, phase):
    wave_y = beam_index[:, 0]
    wave_x = beam_index[:, 1]
    turns = jnp.mod(
        rows_y[:, None] * wave_y[None, :] * FIELD_X + cols_x[:, None] * wave_x[None, :] * FIELD_Y,
        FIELD_Y * FIELD_X,
    )
    angles = phase[None, :] - 2.0 * math.pi / (FIELD_Y * FIELD_X) * turns.astype(jnp.float32)
    real_coef = (amplitude[None, :] * jnp.cos(angles)).astype(jnp.bfloat16)
    imag_coef = (amplitude[None, :] * jnp.sin(angles)).astype(jnp.bfloat16)
    return (real_coef, imag_coef)


def transform_tables():
    counter = np.arange(WIN)
    angles = 2.0 * np.pi / WIN * np.mod(counter[:, None] * counter[None, :], WIN)
    cos_table, sin_table = np.cos(angles) / math.sqrt(WIN), np.sin(angles) / math.sqrt(WIN)
    table = np.block([[cos_table, -sin_table], [sin_table, cos_table]]).astype(np.float32)
    pair = np.stack([table, table.T])
    high = pair.astype(jnp.bfloat16)
    low = (pair - high.astype(np.float32)).astype(jnp.bfloat16)
    return np.stack([high, low], axis=1)


def waves_kernel(oy_ref, ox_ref, coef_ref, s_ref, out_ref, mix_ref, full_ref):
    step = pl.program_id(0)
    outs, depth = coef_ref.shape

    @pl.when(step == 0)
    def _():
        wide = depth * ROWS
        source = lax.broadcasted_iota(jnp.int32, (depth, wide), 0)
        column = lax.broadcasted_iota(jnp.int32, (depth, wide), 1)
        k = column // ROWS
        pick = jnp.where(source == (k % 2) * (depth // 2) + k // 2, 1.0, 0.0).astype(jnp.bfloat16)
        coef = coef_ref[...].astype(jnp.float32)
        tall = jnp.broadcast_to(coef[:, None, :], (outs, ROWS, depth)).reshape(outs * ROWS, depth)
        spread = jnp.dot(tall.astype(jnp.bfloat16), pick, preferred_element_type=jnp.float32)
        row = lax.broadcasted_iota(jnp.int32, (outs * ROWS, wide), 0)
        column = lax.broadcasted_iota(jnp.int32, (outs * ROWS, wide), 1)
        mix_ref[...] = jnp.where(row % ROWS == column % ROWS, spread, 0.0).astype(jnp.bfloat16)

    part = jnp.dot(
        mix_ref[...],
        s_ref[...].reshape(depth * ROWS, FIELD_X),
        preferred_element_type=jnp.float32,
    )
    full_ref[:, pl.ds(pl.multiple_of(step * ROWS, ROWS), ROWS), :] = part.reshape(
        outs, ROWS, FIELD_X
    )

    @pl.when(step == pl.num_programs(0) - 1)
    def _():
        for slot in range(outs // 2):
            up = lax.rem(FIELD_Y - oy_ref[slot], FIELD_Y)
            left = lax.rem(FIELD_X - ox_ref[slot], FIELD_X)
            for plane in range(2):
                rows = pltpu.roll(full_ref[2 * slot + plane], up, 0)[:WIN]
                out_ref[slot, plane] = pltpu.roll(rows, left, 1)[:, :WIN]


def own_waves(s_flat, coef, rows_y, cols_x):
    depth = s_flat.shape[0]
    outs = coef.shape[0]
    return pl.pallas_call(
        waves_kernel,
        grid_spec=pltpu.PrefetchScalarGridSpec(
            num_scalar_prefetch=2,
            grid=(FIELD_Y // ROWS,),
            in_specs=[
                pl.BlockSpec((outs, depth), lambda i, *_: (0, 0)),
                pl.BlockSpec((depth, ROWS, FIELD_X), lambda i, *_: (0, i, 0)),
            ],
            out_specs=pl.BlockSpec((outs // 2, 2, WIN, WIN), lambda i, *_: (0, 0, 0, 0)),
            scratch_shapes=[
                pltpu.VMEM((outs * ROWS, depth * ROWS), jnp.bfloat16),
                pltpu.VMEM((outs, FIELD_Y, FIELD_X), jnp.float32),
            ],
        ),
        out_shape=jax.ShapeDtypeStruct((outs // 2, 2, WIN, WIN), jnp.float32),
        compiler_params=pltpu.CompilerParams(vmem_limit_bytes=LIMIT),
    )(rows_y, cols_x, coef, s_flat)


def split(value):
    high = value.astype(jnp.bfloat16)
    return high, (value - high.astype(jnp.float32)).astype(jnp.bfloat16)


def product(left, right):
    def dot(a, b):
        return jnp.dot(a, b, preferred_element_type=jnp.float32)

    return dot(left[0], right[0]) + (dot(left[1], right[0]) + dot(left[0], right[1]))


def misfit_kernel(info_ref, wave_ref, measured_ref, table_ref, out_ref, field_ref):
    forward = (table_ref[0, 0], table_ref[0, 1])
    inverse = (table_ref[1, 0], table_ref[1, 1])

    def side(value):
        return jnp.concatenate([value[:WIN], value[WIN:]], axis=1)

    def stack(value):
        return jnp.concatenate([value[:, :WIN], value[:, WIN:]], axis=0)

    wave = jnp.concatenate([wave_ref[0], wave_ref[1]], axis=1)
    far = product(inverse, split(stack(product(split(wave), forward))))
    far_real, far_imag = far[:WIN], far[WIN:]
    modulus = jnp.sqrt(far_real * far_real + far_imag * far_imag)
    factor = 1.0 - measured_ref[...] / jnp.maximum(modulus, 0.5)
    resid = jnp.concatenate([far_real * factor, far_imag * factor], axis=0)
    back = product(split(side(product(forward, split(resid)))), inverse)
    back = jnp.concatenate([back, jnp.zeros((FIELD_Y - WIN, 2 * WIN), jnp.float32)], axis=0)
    back = pltpu.roll(back, info_ref[1], 0)
    for plane in range(2):
        field_ref[plane] = back[:, plane * WIN : (plane + 1) * WIN]
    copies = out_ref.shape[1]
    zeros = jnp.zeros((BLOCK - 2 * BAND, WIN), jnp.float32)
    for band in range(BANDS):
        rows = slice(band * BAND, (band + 1) * BAND)
        block = jnp.concatenate([field_ref[0, rows], field_ref[1, rows], zeros], axis=0)
        for copy in range(copies):
            out_ref[band, copy] = block


def misfit_blocks(info, wave, measured, tables, copies):
    return pl.pallas_call(
        misfit_kernel,
        grid_spec=pltpu.PrefetchScalarGridSpec(
            num_scalar_prefetch=1,
            grid=(1,),
            in_specs=[
                pl.BlockSpec((2, WIN, WIN), lambda i, info: (0, 0, 0)),
                pl.BlockSpec((None, WIN, WIN), lambda i, info: (info[0], 0, 0)),
                pl.BlockSpec((2, 2, 2 * WIN, 2 * WIN), lambda i, info: (0, 0, 0, 0)),
            ],
            out_specs=pl.BlockSpec((BANDS, copies, BLOCK, WIN), lambda i, info: (0, 0, 0, 0)),
            scratch_shapes=[pltpu.VMEM((2, FIELD_Y, WIN), jnp.float32)],
        ),
        out_shape=jax.ShapeDtypeStruct((BANDS, copies, BLOCK, WIN), jnp.float32),
        compiler_params=pltpu.CompilerParams(vmem_limit_bytes=LIMIT),
    )(info, wave, measured, tables)


TILE = 8
TILES = -(-BAND // TILE)


def fold_kernel(ox_ref, weight_ref, own_ref, other_ref, out_ref, placed_ref):
    half = own_ref.shape[0]
    depth = weight_ref.shape[1]

    @pl.when(pl.program_id(0) == 0)
    def _():
        blank = jnp.zeros((TILES * TILE, FIELD_X - WIN), jnp.float32)
        for side, ref in enumerate((own_ref, other_ref)):
            for n in range(half):
                shift = ox_ref[side * half + n]
                planes = []
                for plane in range(2):
                    piece = ref[n, plane * BAND : min(plane * BAND + TILES * TILE, BLOCK), :]
                    short = TILES * TILE - piece.shape[0]
                    if short:
                        tail = jnp.zeros((short, WIN), jnp.float32)
                        piece = jnp.concatenate([piece, tail], axis=0)
                    planes.append(pltpu.roll(jnp.concatenate([piece, blank], axis=1), shift, 1))
                for t in range(TILES):
                    rows = slice(t * TILE, (t + 1) * TILE)
                    pair = jnp.concatenate([planes[0][rows], planes[1][rows]], axis=0)
                    at = (side * half + n) * 2 * TILE
                    placed_ref[t, at : at + 2 * TILE, :] = pair.astype(jnp.bfloat16)

    rows, wide = weight_ref.shape[0], depth * TILE
    source = lax.broadcasted_iota(jnp.int32, (depth, wide), 0)
    column = lax.broadcasted_iota(jnp.int32, (depth, wide), 1)
    pick = jnp.where(source == column // TILE, 1.0, 0.0).astype(jnp.bfloat16)
    weight = weight_ref[...].astype(jnp.float32)
    tall = jnp.broadcast_to(weight[:, None, :], (rows, TILE, depth)).reshape(rows * TILE, depth)
    spread = jnp.dot(tall.astype(jnp.bfloat16), pick, preferred_element_type=jnp.float32)
    row = lax.broadcasted_iota(jnp.int32, (rows * TILE, wide), 0)
    column = lax.broadcasted_iota(jnp.int32, (rows * TILE, wide), 1)
    kron = jnp.where(row % TILE == column % TILE, spread, 0.0).astype(jnp.bfloat16)
    for t in range(TILES):
        part = jnp.dot(kron, placed_ref[t], preferred_element_type=jnp.float32)
        part = part.reshape(rows, TILE, FIELD_X)
        left = min(TILE, BAND - t * TILE)
        out_ref[:, t * TILE : t * TILE + left, :] = part[:, :left]


def fold(cols_x, weights, own, other):
    rows, depth = weights.shape
    chunk = rows // 4
    half = own.shape[0]
    return pl.pallas_call(
        fold_kernel,
        grid_spec=pltpu.PrefetchScalarGridSpec(
            num_scalar_prefetch=1,
            grid=(rows // chunk,),
            in_specs=[
                pl.BlockSpec((chunk, depth), lambda i, *_: (i, 0)),
                pl.BlockSpec((half, BLOCK, WIN), lambda i, *_: (0, 0, 0)),
                pl.BlockSpec((half, BLOCK, WIN), lambda i, *_: (0, 0, 0)),
            ],
            out_specs=pl.BlockSpec((chunk, BAND, FIELD_X), lambda i, *_: (i, 0, 0)),
            scratch_shapes=[pltpu.VMEM((TILES, depth * TILE, FIELD_X), jnp.bfloat16)],
        ),
        out_shape=jax.ShapeDtypeStruct((rows, BAND, FIELD_X), jnp.float32),
        compiler_params=pltpu.CompilerParams(vmem_limit_bytes=LIMIT),
    )(cols_x, weights, own, other)


def swap(value, axis, pairs):
    both = [(a, b) for a, b in pairs] + [(b, a) for a, b in pairs]
    return lax.ppermute(value, axis, both)


def body(s_matrix, beam_index, amplitude, phase, offsets_y, offsets_x, measured):
    local_count = measured.shape[0]
    beams_here = s_matrix.shape[0]
    group = lax.axis_index("pos")
    core = lax.axis_index("core")
    lane = lax.axis_index("yl")
    depth = lax.axis_size("z")

    def slots(offsets):
        own = lax.dynamic_slice_in_dim(offsets, group * local_count, local_count).reshape(2, 2)
        own = jnp.where(core == 1, own[::-1], own)
        own = jnp.where(lane == 1, own[:, ::-1], own)
        return own.reshape(-1)

    own_y, own_x = slots(offsets_y), slots(offsets_x)
    real_coef, imag_coef = beam_weights(own_y, own_x, beam_index, amplitude, phase)
    upper = jnp.concatenate([real_coef, -imag_coef], axis=1)
    lower = jnp.concatenate([imag_coef, real_coef], axis=1)
    coef = jnp.stack([upper, lower], axis=1).reshape(2 * local_count, 2 * beams_here)
    s_flat = s_matrix.reshape(beams_here * 2, FIELD_Y, FIELD_X)
    waves = own_waves(s_flat, coef, own_y, own_x)

    pair = waves[:2] + swap(waves[2:], "core", [(0, 1)])
    total = pair[0] + swap(pair[1], "yl", [(0, 1)])
    for bit in (1, 2):
        total = total + swap(total, "z", [(i, i ^ bit) for i in range(depth) if not i & bit])
    total = total + swap(total, "z", [(i, depth - 1 - i) for i in range(depth // 2)])

    info = jnp.stack([2 * core + lane, own_y[0]]).astype(jnp.int32)
    copies = lax.axis_size("yl")
    blocks = misfit_blocks(info, total, measured, jnp.asarray(transform_tables()), copies)
    blocks = blocks.reshape(BANDS * copies, BLOCK, WIN)
    received = lax.all_to_all(blocks, ("pos", "yl"), 0, 0, tiled=True)
    other = swap(received, "core", [(0, 1)])

    def order(offsets):
        sides = offsets.reshape(BANDS, 2, 2).transpose(1, 0, 2)
        return jnp.where(core == 1, sides[::-1], sides).reshape(-1)

    all_y, all_x = order(offsets_y), order(offsets_x)
    real_coef, imag_coef = beam_weights(all_y, all_x, beam_index, amplitude, phase)
    real_coef, imag_coef = real_coef.T, imag_coef.T
    upper = jnp.stack([real_coef, imag_coef], axis=-1)
    lower = jnp.stack([-imag_coef, real_coef], axis=-1)
    weights = jnp.stack([upper, lower], axis=1).reshape(2 * beams_here, -1)
    gradient = fold(all_x, weights, received, other)
    return gradient.reshape(beams_here, 2, BAND, FIELD_X)


def solution(mesh):
    fine = Mesh(mesh.devices.reshape(8, 8, 2, 2), ("pos", "z", "yl", "core"))
    beam = ("z", "yl", "core")
    return jax.shard_map(
        body,
        mesh=fine,
        in_specs=(
            P(beam, None, None, None),
            P(beam, None),
            P(beam),
            P(beam),
            P(),
            P(),
            P("pos", None, None),
        ),
        out_specs=P(beam, None, "pos", None),
        check_vma=False,
    )
```

```python
import math

import jax
import jax.numpy as jnp
import numpy as np
from jax import lax
from jax.experimental import pallas as pl
from jax.experimental.pallas import tpu as pltpu
from jax.sharding import Mesh
from jax.sharding import PartitionSpec as P

WIN = 128
FIELD_Y = 144
FIELD_X = 256
BANDS = 8
BAND = FIELD_Y // BANDS
BLOCK = 40
ROWS = 16
LIMIT = 48 * 1024 * 1024
WHOLE = 60 * 1024 * 1024


def beam_weights(rows_y, cols_x, beams):
    wave_y, wave_x, amplitude, phase = beams
    cells = FIELD_Y * FIELD_X
    count = rows_y * wave_y * FIELD_X + cols_x * wave_x * FIELD_Y
    whole = jnp.floor(count.astype(jnp.float32) * (1.0 / cells)).astype(jnp.int32)
    turns = count - whole * cells
    turns = jnp.where(turns < 0, turns + cells, turns)
    turns = jnp.where(turns >= cells, turns - cells, turns)
    angles = phase - 2.0 * math.pi / cells * turns.astype(jnp.float32)
    return amplitude * jnp.cos(angles), amplitude * jnp.sin(angles)


def places(count, offset_of, shape):
    row = lax.broadcasted_iota(jnp.int32, shape, 0)
    value = jnp.zeros(shape, jnp.int32)
    for n in range(count):
        value = jnp.where(row == n, offset_of(n), value)
    return value


def one_hot(condition):
    return jnp.where(condition, 1.0, 0.0).astype(jnp.bfloat16)


def iota2(shape):
    return [lax.broadcasted_iota(jnp.int32, shape, axis) for axis in range(2)]


def dot(left, right):
    return jnp.dot(left, right, preferred_element_type=jnp.float32)


def transform_tables():
    counter = np.arange(WIN)
    angles = 2.0 * np.pi / WIN * np.mod(counter[:, None] * counter[None, :], WIN)
    cos_table, sin_table = np.cos(angles) / math.sqrt(WIN), np.sin(angles) / math.sqrt(WIN)
    table = np.block([[cos_table, -sin_table], [sin_table, cos_table]]).astype(np.float32)
    pair = np.stack([table, table.T])
    high = pair.astype(jnp.bfloat16)
    low = (pair - high.astype(np.float32)).astype(jnp.bfloat16)
    return np.stack([high, low], axis=1)


def slot_position(slot):
    core = lax.axis_index("core") ^ (slot // 2)
    lane = lax.axis_index("yl") ^ (slot % 2)
    return lax.axis_index("pos") * 4 + 2 * core + lane


GROUPS = ((0, 6), (6, 9))


def waves_kernel(
    oy_hbm, ox_hbm, index_hbm, amplitude_hbm, phase_hbm, s_hbm,
    keep_ref, send_ref,
    oy_ref, ox_ref, index_ref, amplitude_ref, phase_ref, s_ref, mix_ref, full_ref, part_ref, small_sem, tile_sem,
):
    depth, tiles = s_ref.shape[0], FIELD_Y // ROWS
    beams = depth // 2
    small = [
        pltpu.make_async_copy(source, target, small_sem.at[i])
        for i, (source, target) in enumerate(
            [
                (oy_hbm, oy_ref),
                (ox_hbm, ox_ref),
                (index_hbm, index_ref),
                (amplitude_hbm, amplitude_ref),
                (phase_hbm, phase_ref),
            ]
        )
    ]
    large = []
    for i in range(tiles):
        rows = pl.ds(i * ROWS, ROWS)
        large.append(pltpu.make_async_copy(s_hbm.at[:, rows], s_ref.at[:, rows], tile_sem.at[i]))
    for copy in small + large:
        copy.start()

    outs, wide = 8, depth * ROWS
    source, column = iota2((beams, wide))
    same = source == column // (2 * ROWS)
    first = column % (2 * ROWS) < ROWS
    picks = [one_hot(same & first), one_hot(same & ~first)]
    for copy in small:
        copy.wait()
    slots = [slot_position(slot) for slot in range(4)]
    shape = (outs, beams)
    rows_y = places(outs, lambda n: oy_ref[slots[n // 2]], shape)
    cols_x = places(outs, lambda n: ox_ref[slots[n // 2]], shape)
    waves = [index_ref[0:1], index_ref[1:2], amplitude_ref[...], phase_ref[...]]
    real, imag = beam_weights(rows_y, cols_x, waves)
    is_real = iota2(shape)[0] % 2 == 0
    spread = jnp.zeros((outs * ROWS, wide), jnp.float32)
    for coef, pick in zip(
        (jnp.where(is_real, real, imag), jnp.where(is_real, -imag, real)), picks, strict=True
    ):
        tall = jnp.broadcast_to(coef[:, None, :], (outs, ROWS, beams)).reshape(outs * ROWS, beams)
        spread += dot(tall.astype(jnp.bfloat16), pick)
    row = lax.broadcasted_iota(jnp.int32, (outs * ROWS, 1), 0)
    moved = row
    for slot in range(4):
        moved += jnp.where(row // (2 * ROWS) == slot, oy_ref[slots[slot]], 0)
    column = iota2((outs * ROWS, wide))[1]
    mix_ref[...] = jnp.where(moved % ROWS == column % ROWS, spread, 0.0).astype(jnp.bfloat16)

    lefts = [lax.rem(FIELD_X - ox_ref[slots[slot]], FIELD_X) for slot in range(4)]

    def multiply(span):
        for i in range(*span):
            tile = s_ref[:, i * ROWS : (i + 1) * ROWS, :].reshape(wide, FIELD_X)
            full_ref[i] = dot(mix_ref[...], tile)

    def crop(span):
        for i in range(*span):
            for slot in range(4):
                both = full_ref[i, 2 * slot * ROWS : 2 * (slot + 1) * ROWS]
                part_ref[slot, i] = pltpu.roll(both, lefts[slot], 1)[:, :WIN]
        low, high = max(span[0] - 2, 0), span[1] - 2
        if span[1] == tiles:
            high = WIN // ROWS
        for slot in range(4):
            offset = oy_ref[slots[slot]]
            skip, rest = offset // ROWS, ROWS - offset % ROWS
            upper = iota2((2 * ROWS, WIN))[0] % ROWS < rest
            ref = (keep_ref, send_ref)[slot // 2]
            for u in range(low, high):
                after = jnp.minimum(u + skip + 1, tiles - 1)
                value = jnp.where(upper, part_ref[slot, u + skip], part_ref[slot, after])
                for plane in range(2):
                    rows = slice(u * ROWS, (u + 1) * ROWS)
                    ref[slot % 2, plane, rows] = value[plane * ROWS : (plane + 1) * ROWS]

    for number, span in enumerate(GROUPS):
        for i in range(*span):
            large[i].wait()
        multiply(span)
        if number:
            crop(GROUPS[number - 1])
    crop(GROUPS[-1])


def own_waves(s_flat, offsets_y, offsets_x, beams):
    depth = s_flat.shape[0]
    half = pltpu.VMEM((2, 2, WIN, WIN), jnp.float32)
    small = (offsets_y, offsets_x, *beams)
    operands = (*small, s_flat)
    return pl.pallas_call(
        waves_kernel,
        in_specs=[pl.BlockSpec(memory_space=pl.ANY)] * len(operands),
        out_specs=[pl.BlockSpec(memory_space=pltpu.VMEM)] * 2,
        out_shape=[half, half],
        scratch_shapes=[
            pltpu.SMEM(offsets_y.shape, jnp.int32),
            pltpu.SMEM(offsets_x.shape, jnp.int32),
            *[pltpu.VMEM(array.shape, array.dtype) for array in beams],
            pltpu.VMEM(s_flat.shape, s_flat.dtype),
            pltpu.VMEM((8 * ROWS, depth * ROWS), jnp.bfloat16),
            pltpu.VMEM((FIELD_Y // ROWS, 8 * ROWS, FIELD_X), jnp.float32),
            pltpu.VMEM((4, FIELD_Y // ROWS, 2 * ROWS, WIN), jnp.float32),
            pltpu.SemaphoreType.DMA((len(small),)),
            pltpu.SemaphoreType.DMA((FIELD_Y // ROWS,)),
        ],
        compiler_params=pltpu.CompilerParams(vmem_limit_bytes=WHOLE),
    )(*operands)


def split(value):
    high = value.astype(jnp.bfloat16)
    return high, (value - high.astype(jnp.float32)).astype(jnp.bfloat16)


def product(left, right):
    return dot(left[0], right[0]) + (dot(left[1], right[0]) + dot(left[0], right[1]))


def misfit_kernel(oy_ref, wave_ref, measured_ref, table_ref, out_ref, field_ref):
    forward = (table_ref[0, 0], table_ref[0, 1])
    inverse = (table_ref[1, 0], table_ref[1, 1])

    def side(value):
        return jnp.concatenate([value[:WIN], value[WIN:]], axis=1)

    def stack(value):
        return jnp.concatenate([value[:, :WIN], value[:, WIN:]], axis=0)

    wave = jnp.concatenate([wave_ref[0], wave_ref[1]], axis=1)
    far = product(inverse, split(stack(product(split(wave), forward))))
    far_real, far_imag = far[:WIN], far[WIN:]
    modulus = jnp.sqrt(far_real * far_real + far_imag * far_imag)
    factor = 1.0 - measured_ref[lax.rem(slot_position(0), 4)] / jnp.maximum(modulus, 0.5)
    resid = jnp.concatenate([far_real * factor, far_imag * factor], axis=0)
    back = product(split(side(product(forward, split(resid)))), inverse)
    back = jnp.concatenate([back, jnp.zeros((FIELD_Y - WIN, 2 * WIN), jnp.float32)], axis=0)
    back = pltpu.roll(back, oy_ref[slot_position(0)], 0)
    for plane in range(2):
        field_ref[plane] = back[:, plane * WIN : (plane + 1) * WIN]
    copies = out_ref.shape[1]
    zeros = jnp.zeros((BLOCK - 2 * BAND, WIN), jnp.float32)
    for band in range(BANDS):
        rows = slice(band * BAND, (band + 1) * BAND)
        block = jnp.concatenate([field_ref[0, rows], field_ref[1, rows], zeros], axis=0)
        for copy in range(copies):
            out_ref[band, copy] = block


def misfit_blocks(offsets_y, wave, measured, tables, copies):
    return pl.pallas_call(
        misfit_kernel,
        in_specs=[pl.BlockSpec(memory_space=pltpu.SMEM)] + [pl.BlockSpec(memory_space=pltpu.VMEM)] * 3,
        out_specs=pl.BlockSpec(memory_space=pltpu.VMEM),
        scratch_shapes=[pltpu.VMEM((2, FIELD_Y, WIN), jnp.float32)],
        out_shape=jax.ShapeDtypeStruct((BANDS, copies, BLOCK, WIN), jnp.float32),
        compiler_params=pltpu.CompilerParams(vmem_limit_bytes=LIMIT),
    )(offsets_y, wave, measured, tables)


TILE = 8
FULL = BAND // TILE
REST = BAND - FULL * TILE
HALF = 16
LINES = 2 * FIELD_X // WIN


def side_position(side, n):
    core = lax.axis_index("core") ^ side
    return n // 2 * 4 + 2 * core + n % 2


def spread_weights(coefs, size, row_parts, shape):
    count, beams = coefs[0].shape
    beam, plane, _ = row_parts((shape[0], beams))
    pick = one_hot(beam == iota2((shape[0], beams))[1])
    real, imag = [
        lax.dot_general(pick, coef, (((1,), (1,)), ((), ())), preferred_element_type=jnp.float32)
        for coef in coefs
    ]
    first = row_parts((shape[0], count))[1] == 0
    source, column = iota2((count, shape[1]))
    same = source == column // (2 * size)
    low = column % (2 * size) < size
    spread = dot(jnp.where(first, real, -imag).astype(jnp.bfloat16), one_hot(same & low))
    spread += dot(jnp.where(first, imag, real).astype(jnp.bfloat16), one_hot(same & ~low))
    equal = row_parts(shape)[2] == iota2(shape)[1] % size
    return jnp.where(equal, spread, 0.0).astype(jnp.bfloat16)


def weights_kernel(oy_ref, ox_ref, index_ref, amplitude_ref, phase_ref, full_ref, rest_ref):
    beams, count = index_ref.shape[1], 2 * HALF
    where = [side_position(n // HALF, n % HALF) for n in range(count)]
    shape = (count, beams)
    rows_y = places(count, lambda n: oy_ref[where[n]], shape)
    cols_x = places(count, lambda n: ox_ref[where[n]], shape)
    waves = [index_ref[0:1], index_ref[1:2], amplitude_ref[...], phase_ref[...]]
    coefs = [value.astype(jnp.bfloat16) for value in beam_weights(rows_y, cols_x, waves)]

    def full_parts(shape):
        row = iota2(shape)[0]
        return row // (2 * TILE), row // TILE % 2, row % TILE

    def rest_parts(shape):
        row = iota2(shape)[0]
        return row % beams, row // (beams * REST), row // beams % REST

    full_ref[...] = spread_weights(coefs, TILE, full_parts, full_ref.shape)
    rest_ref[...] = spread_weights(coefs, REST, rest_parts, rest_ref.shape)


def fold_weights(offsets_y, offsets_x, beams):
    rows, columns = 2 * beams[1].shape[1], 4 * HALF
    shapes = [(rows * size, columns * size) for size in (TILE, REST)]
    return pl.pallas_call(
        weights_kernel,
        in_specs=[pl.BlockSpec(memory_space=pltpu.SMEM)] * 2 + [pl.BlockSpec(memory_space=pltpu.VMEM)] * 3,
        out_specs=[pl.BlockSpec(memory_space=pltpu.VMEM)] * 2,
        out_shape=[jax.ShapeDtypeStruct(shape, jnp.bfloat16) for shape in shapes],
        compiler_params=pltpu.CompilerParams(vmem_limit_bytes=LIMIT),
        cost_estimate=pl.CostEstimate(flops=100000000, bytes_accessed=1000000, transcendentals=0),
    )(offsets_y, offsets_x, *beams)


PLACED = [(FULL, 2 * HALF * TILE, FIELD_X), (2 * HALF * REST, FIELD_X)]


def place(side, ox_ref, received_ref, full_ref, rest_ref):
    blank = jnp.zeros((2 * BAND, FIELD_X - WIN), jnp.float32)
    tails = []
    for n in range(HALF):
        shift = ox_ref[side_position(side, n)]
        both = jnp.concatenate([received_ref[n, : 2 * BAND, :], blank], axis=1)
        both = pltpu.roll(both, shift, 1)
        planes = [both[:BAND], both[BAND:]]
        for t in range(FULL):
            rows = slice(t * TILE, (t + 1) * TILE)
            pair = jnp.concatenate([planes[0][rows], planes[1][rows]], axis=0)
            full_ref[t, n * 2 * TILE : (n + 1) * 2 * TILE, :] = pair.astype(jnp.bfloat16)
        tails += [plane[FULL * TILE :] for plane in planes]
    rest_ref[...] = jnp.concatenate(tails, axis=0).astype(jnp.bfloat16)


def place_kernel(ox_ref, received_ref, full_ref, rest_ref):
    place(0, ox_ref, received_ref, full_ref, rest_ref)


def place_own(offsets_x, received):
    return pl.pallas_call(
        place_kernel,
        in_specs=[pl.BlockSpec(memory_space=pltpu.SMEM), pl.BlockSpec(memory_space=pltpu.VMEM)],
        out_specs=[pl.BlockSpec(memory_space=pltpu.VMEM)] * 2,
        out_shape=[jax.ShapeDtypeStruct(shape, jnp.bfloat16) for shape in PLACED],
        compiler_params=pltpu.CompilerParams(vmem_limit_bytes=LIMIT),
        cost_estimate=pl.CostEstimate(flops=1000000, bytes_accessed=1000000, transcendentals=0),
    )(offsets_x, received)


CHUNKS = 4


def fold_kernel(
    ox_ref, weight_ref, weight_rest_ref, own_ref, own_rest_ref, other_ref,
    out_hbm,
    full_ref, rest_ref, line_ref, sem,
):
    place(1, ox_ref, other_ref, full_ref, rest_ref)
    beams = weight_ref.shape[0] // (2 * TILE)
    length = BAND * LINES
    columns = [slice(side * WIN, (side + 1) * WIN) for side in range(FIELD_X // WIN)]

    half = own_rest_ref.shape[0]
    part = dot(weight_rest_ref[:, :half], own_rest_ref[...])
    part += dot(weight_rest_ref[:, half:], rest_ref[...])
    for group in range(2 * REST):
        plane, y = divmod(group, REST)
        value = part[group * beams : (group + 1) * beams]
        for side, column in enumerate(columns):
            start = (FULL * TILE + y) * LINES + 2 * side + plane
            line_ref[pl.ds(start, beams, stride=length), :] = value[:, column]

    half = own_ref.shape[1]
    rows, lines = weight_ref.shape[0] // CHUNKS, beams * length // CHUNKS
    copies = []
    for chunk in range(CHUNKS):
        for t in range(FULL):
            at = slice(chunk * rows, (chunk + 1) * rows)
            part = dot(weight_ref[at, :half], own_ref[t]) + dot(weight_ref[at, half:], full_ref[t])
            for group in range(rows // TILE):
                beam, plane = divmod(group, 2)
                value = part[group * TILE : (group + 1) * TILE]
                for side, column in enumerate(columns):
                    start = chunk * lines + beam * length + t * TILE * LINES + 2 * side + plane
                    line_ref[pl.ds(start, TILE, stride=LINES), :] = value[:, column]
        at = pl.ds(chunk * lines, lines)
        copy = pltpu.make_async_copy(line_ref.at[at], out_hbm.at[at], sem.at[chunk])
        copy.start()
        copies.append(copy)
    for copy in copies:
        copy.wait()


def fold(offsets_x, weights, own, other):
    lines = weights[0].shape[0] // (2 * TILE) * BAND * LINES
    operands = (*weights, *own, other)
    return pl.pallas_call(
        fold_kernel,
        in_specs=[pl.BlockSpec(memory_space=pltpu.SMEM)] + [pl.BlockSpec(memory_space=pltpu.VMEM)] * len(operands),
        out_specs=pl.BlockSpec(memory_space=pl.ANY),
        out_shape=jax.ShapeDtypeStruct((lines, WIN), jnp.float32),
        scratch_shapes=[
            *[pltpu.VMEM(shape, jnp.bfloat16) for shape in PLACED],
            pltpu.VMEM((lines, WIN), jnp.float32),
            pltpu.SemaphoreType.DMA((CHUNKS,)),
        ],
        compiler_params=pltpu.CompilerParams(vmem_limit_bytes=LIMIT),
    )(offsets_x, *operands)


def swap(value, axis, pairs):
    both = [(a, b) for a, b in pairs] + [(b, a) for a, b in pairs]
    return lax.ppermute(value, axis, both)


def body(s_matrix, beam_index, amplitude, phase, offsets_y, offsets_x, measured):
    beams_here = s_matrix.shape[0]
    depth = lax.axis_size("z")
    beams = (beam_index.T, amplitude[None, :], phase[None, :])
    s_flat = s_matrix.reshape(beams_here * 2, FIELD_Y, FIELD_X)

    keep, send = own_waves(s_flat, offsets_y, offsets_x, beams)
    pair = keep + swap(send, "core", [(0, 1)])
    total = pair[0] + swap(pair[1], "yl", [(0, 1)])
    weights = fold_weights(offsets_y, offsets_x, beams)
    for bit in (1, 2):
        other = swap(total, "z", [(i, i ^ bit) for i in range(depth) if not i & bit])
        if bit == 1:
            other, weights = lax.optimization_barrier((other, weights))
        total = total + other
    total = total + swap(total, "z", [(i, depth - 1 - i) for i in range(depth // 2)])

    copies = lax.axis_size("yl")
    blocks = misfit_blocks(offsets_y, total, measured, jnp.asarray(transform_tables()), copies)
    blocks = blocks.reshape(BANDS * copies, BLOCK, WIN)
    received = lax.all_to_all(blocks, ("pos", "yl"), 0, 0, tiled=True)
    other = swap(received, "core", [(0, 1)])
    own = place_own(offsets_x, received)
    lines = fold(offsets_x, weights, own, other)
    gradient = lines.reshape(beams_here, BAND, FIELD_X // WIN, 2, WIN).transpose(0, 3, 1, 2, 4)
    return gradient.reshape(beams_here, 2, BAND, FIELD_X)


def solution(mesh):
    fine = Mesh(mesh.devices.reshape(8, 8, 2, 2), ("pos", "z", "yl", "core"))
    beam = ("z", "yl", "core")
    return jax.shard_map(
        body,
        mesh=fine,
        in_specs=(
            P(beam, None, None, None),
            P(beam, None),
            P(beam),
            P(beam),
            P(),
            P(),
            P("pos", None, None),
        ),
        out_specs=P(beam, None, "pos", None),
        check_vma=False,
    )
```

```python
import math

import jax
import jax.numpy as jnp
import numpy as np
from jax import lax
from jax.experimental import pallas as pl
from jax.experimental.pallas import tpu as pltpu
from jax.sharding import Mesh
from jax.sharding import PartitionSpec as P

WIN = 128
FIELD_Y = 144
FIELD_X = 256
BANDS = 8
BAND = FIELD_Y // BANDS
BLOCK = 40
ROWS = 16
LIMIT = 48 * 1024 * 1024
WHOLE = 60 * 1024 * 1024


def beam_weights(rows_y, cols_x, beams):
    wave_y, wave_x, amplitude, phase = beams
    cells = FIELD_Y * FIELD_X
    count = rows_y * wave_y * FIELD_X + cols_x * wave_x * FIELD_Y
    whole = jnp.floor(count.astype(jnp.float32) * (1.0 / cells)).astype(jnp.int32)
    turns = count - whole * cells
    turns = jnp.where(turns < 0, turns + cells, turns)
    turns = jnp.where(turns >= cells, turns - cells, turns)
    angles = phase - 2.0 * math.pi / cells * turns.astype(jnp.float32)
    return amplitude * jnp.cos(angles), amplitude * jnp.sin(angles)


def places(count, offset_of, shape):
    row = lax.broadcasted_iota(jnp.int32, shape, 0)
    value = jnp.zeros(shape, jnp.int32)
    for n in range(count):
        value = jnp.where(row == n, offset_of(n), value)
    return value


def one_hot(condition):
    return jnp.where(condition, 1.0, 0.0).astype(jnp.bfloat16)


def iota2(shape):
    return [lax.broadcasted_iota(jnp.int32, shape, axis) for axis in range(2)]


def dot(left, right):
    return jnp.dot(left, right, preferred_element_type=jnp.float32)


def transform_tables():
    counter = np.arange(WIN)
    angles = 2.0 * np.pi / WIN * np.mod(counter[:, None] * counter[None, :], WIN)
    cos_table, sin_table = np.cos(angles) / math.sqrt(WIN), np.sin(angles) / math.sqrt(WIN)
    table = np.block([[cos_table, -sin_table], [sin_table, cos_table]]).astype(np.float32)
    pair = np.stack([table, table.T])
    high = pair.astype(jnp.bfloat16)
    low = (pair - high.astype(np.float32)).astype(jnp.bfloat16)
    return np.stack([high, low], axis=1)


def slot_position(slot):
    core = lax.axis_index("core") ^ (slot // 2)
    lane = lax.axis_index("yl") ^ (slot % 2)
    return lax.axis_index("pos") * 4 + 2 * core + lane


GROUPS = ((0, 5), (5, 9))


def waves_kernel(
    oy_hbm, ox_hbm, index_hbm, amplitude_hbm, phase_hbm, s_hbm,
    keep_ref, send_ref,
    oy_ref, ox_ref, index_ref, amplitude_ref, phase_ref, s_ref, mix_ref, full_ref, part_ref, small_sem, tile_sem,
):
    depth, tiles = s_ref.shape[0], FIELD_Y // ROWS
    beams = depth // 2
    small = [
        pltpu.make_async_copy(source, target, small_sem.at[i])
        for i, (source, target) in enumerate(
            [
                (oy_hbm, oy_ref),
                (ox_hbm, ox_ref),
                (index_hbm, index_ref),
                (amplitude_hbm, amplitude_ref),
                (phase_hbm, phase_ref),
            ]
        )
    ]
    large = []
    for i in range(tiles):
        rows = pl.ds(i * ROWS, ROWS)
        large.append(pltpu.make_async_copy(s_hbm.at[:, rows], s_ref.at[:, rows], tile_sem.at[i]))
    for copy in small + large[: GROUPS[0][1]]:
        copy.start()
    for copy in large[GROUPS[0][1] :]:
        copy.start(priority=1)

    outs, wide = 8, depth * ROWS
    source, column = iota2((beams, wide))
    same = source == column // (2 * ROWS)
    first = column % (2 * ROWS) < ROWS
    picks = [one_hot(same & first), one_hot(same & ~first)]
    for copy in small:
        copy.wait()
    slots = [slot_position(slot) for slot in range(4)]
    shape = (outs, beams)
    rows_y = places(outs, lambda n: oy_ref[slots[n // 2]], shape)
    cols_x = places(outs, lambda n: ox_ref[slots[n // 2]], shape)
    waves = [index_ref[0:1], index_ref[1:2], amplitude_ref[...], phase_ref[...]]
    real, imag = beam_weights(rows_y, cols_x, waves)
    is_real = iota2(shape)[0] % 2 == 0
    spread = jnp.zeros((outs * ROWS, wide), jnp.float32)
    for coef, pick in zip(
        (jnp.where(is_real, real, imag), jnp.where(is_real, -imag, real)), picks, strict=True
    ):
        tall = jnp.broadcast_to(coef[:, None, :], (outs, ROWS, beams)).reshape(outs * ROWS, beams)
        spread += dot(tall.astype(jnp.bfloat16), pick)
    row = lax.broadcasted_iota(jnp.int32, (outs * ROWS, 1), 0)
    moved = row
    for slot in range(4):
        moved += jnp.where(row // (2 * ROWS) == slot, oy_ref[slots[slot]], 0)
    column = iota2((outs * ROWS, wide))[1]
    mix_ref[...] = jnp.where(moved % ROWS == column % ROWS, spread, 0.0).astype(jnp.bfloat16)

    lefts = [lax.rem(FIELD_X - ox_ref[slots[slot]], FIELD_X) for slot in range(4)]

    def multiply(span):
        for i in range(*span):
            tile = s_ref[:, i * ROWS : (i + 1) * ROWS, :].reshape(wide, FIELD_X)
            full_ref[i] = dot(mix_ref[...], tile)

    def crop(span):
        for i in range(*span):
            for slot in range(4):
                both = full_ref[i, 2 * slot * ROWS : 2 * (slot + 1) * ROWS]
                part_ref[slot, i] = pltpu.roll(both, lefts[slot], 1)[:, :WIN]
        low, high = max(span[0] - 2, 0), span[1] - 2
        if span[1] == tiles:
            high = WIN // ROWS
        for slot in range(4):
            offset = oy_ref[slots[slot]]
            skip, rest = offset // ROWS, ROWS - offset % ROWS
            upper = iota2((2 * ROWS, WIN))[0] % ROWS < rest
            ref = (keep_ref, send_ref)[slot // 2]
            for u in range(low, high):
                after = jnp.minimum(u + skip + 1, tiles - 1)
                value = jnp.where(upper, part_ref[slot, u + skip], part_ref[slot, after])
                for plane in range(2):
                    rows = slice(u * ROWS, (u + 1) * ROWS)
                    ref[slot % 2, plane, rows] = value[plane * ROWS : (plane + 1) * ROWS]

    for number, span in enumerate(GROUPS):
        for i in range(*span):
            large[i].wait()
        multiply(span)
        if number:
            crop(GROUPS[number - 1])
    crop(GROUPS[-1])


def own_waves(s_flat, offsets_y, offsets_x, beams):
    depth = s_flat.shape[0]
    half = pltpu.VMEM((2, 2, WIN, WIN), jnp.float32)
    small = (offsets_y, offsets_x, *beams)
    operands = (*small, s_flat)
    return pl.pallas_call(
        waves_kernel,
        in_specs=[pl.BlockSpec(memory_space=pl.ANY)] * len(operands),
        out_specs=[pl.BlockSpec(memory_space=pltpu.VMEM)] * 2,
        out_shape=[half, half],
        scratch_shapes=[
            pltpu.SMEM(offsets_y.shape, jnp.int32),
            pltpu.SMEM(offsets_x.shape, jnp.int32),
            *[pltpu.VMEM(array.shape, array.dtype) for array in beams],
            pltpu.VMEM(s_flat.shape, s_flat.dtype),
            pltpu.VMEM((8 * ROWS, depth * ROWS), jnp.bfloat16),
            pltpu.VMEM((FIELD_Y // ROWS, 8 * ROWS, FIELD_X), jnp.float32),
            pltpu.VMEM((4, FIELD_Y // ROWS, 2 * ROWS, WIN), jnp.float32),
            pltpu.SemaphoreType.DMA((len(small),)),
            pltpu.SemaphoreType.DMA((FIELD_Y // ROWS,)),
        ],
        compiler_params=pltpu.CompilerParams(vmem_limit_bytes=WHOLE),
    )(*operands)


def split(value):
    high = value.astype(jnp.bfloat16)
    return high, (value - high.astype(jnp.float32)).astype(jnp.bfloat16)


def product(left, right):
    return dot(left[0], right[0]) + (dot(left[1], right[0]) + dot(left[0], right[1]))


def misfit_kernel(oy_ref, wave_ref, measured_ref, table_ref, out_ref, field_ref):
    forward = (table_ref[0, 0], table_ref[0, 1])
    inverse = (table_ref[1, 0], table_ref[1, 1])

    def side(value):
        return jnp.concatenate([value[:WIN], value[WIN:]], axis=1)

    def stack(value):
        return jnp.concatenate([value[:, :WIN], value[:, WIN:]], axis=0)

    wave = jnp.concatenate([wave_ref[0], wave_ref[1]], axis=1)
    far = product(inverse, split(stack(product(split(wave), forward))))
    far_real, far_imag = far[:WIN], far[WIN:]
    modulus = jnp.sqrt(far_real * far_real + far_imag * far_imag)
    factor = 1.0 - measured_ref[lax.rem(slot_position(0), 4)] / jnp.maximum(modulus, 0.5)
    resid = jnp.concatenate([far_real * factor, far_imag * factor], axis=0)
    back = product(split(side(product(forward, split(resid)))), inverse)
    back = jnp.concatenate([back, jnp.zeros((FIELD_Y - WIN, 2 * WIN), jnp.float32)], axis=0)
    back = pltpu.roll(back, oy_ref[slot_position(0)], 0)
    for plane in range(2):
        field_ref[plane] = back[:, plane * WIN : (plane + 1) * WIN]
    copies = out_ref.shape[1]
    zeros = jnp.zeros((BLOCK - 2 * BAND, WIN), jnp.float32)
    for band in range(BANDS):
        rows = slice(band * BAND, (band + 1) * BAND)
        block = jnp.concatenate([field_ref[0, rows], field_ref[1, rows], zeros], axis=0)
        for copy in range(copies):
            out_ref[band, copy] = block


def misfit_blocks(offsets_y, wave, measured, tables, copies):
    return pl.pallas_call(
        misfit_kernel,
        in_specs=[pl.BlockSpec(memory_space=pltpu.SMEM)] + [pl.BlockSpec(memory_space=pltpu.VMEM)] * 3,
        out_specs=pl.BlockSpec(memory_space=pltpu.VMEM),
        scratch_shapes=[pltpu.VMEM((2, FIELD_Y, WIN), jnp.float32)],
        out_shape=jax.ShapeDtypeStruct((BANDS, copies, BLOCK, WIN), jnp.float32),
        compiler_params=pltpu.CompilerParams(vmem_limit_bytes=LIMIT),
    )(offsets_y, wave, measured, tables)


TILE = 8
FULL = BAND // TILE
REST = BAND - FULL * TILE
HALF = 16
LINES = 2 * FIELD_X // WIN


def side_position(side, n):
    core = lax.axis_index("core") ^ side
    return n // 2 * 4 + 2 * core + n % 2


def spread_weights(coefs, size, row_parts, shape):
    count, beams = coefs[0].shape
    beam, plane, _ = row_parts((shape[0], beams))
    pick = one_hot(beam == iota2((shape[0], beams))[1])
    real, imag = [
        lax.dot_general(pick, coef, (((1,), (1,)), ((), ())), preferred_element_type=jnp.float32)
        for coef in coefs
    ]
    first = row_parts((shape[0], count))[1] == 0
    source, column = iota2((count, shape[1]))
    same = source == column // (2 * size)
    low = column % (2 * size) < size
    spread = dot(jnp.where(first, real, -imag).astype(jnp.bfloat16), one_hot(same & low))
    spread += dot(jnp.where(first, imag, real).astype(jnp.bfloat16), one_hot(same & ~low))
    equal = row_parts(shape)[2] == iota2(shape)[1] % size
    return jnp.where(equal, spread, 0.0).astype(jnp.bfloat16)


def weights_kernel(oy_ref, ox_ref, index_ref, amplitude_ref, phase_ref, full_ref, rest_ref):
    beams, count = index_ref.shape[1], 2 * HALF
    where = [side_position(n // HALF, n % HALF) for n in range(count)]
    shape = (count, beams)
    rows_y = places(count, lambda n: oy_ref[where[n]], shape)
    cols_x = places(count, lambda n: ox_ref[where[n]], shape)
    waves = [index_ref[0:1], index_ref[1:2], amplitude_ref[...], phase_ref[...]]
    coefs = [value.astype(jnp.bfloat16) for value in beam_weights(rows_y, cols_x, waves)]

    def full_parts(shape):
        row = iota2(shape)[0]
        return row // (2 * TILE), row // TILE % 2, row % TILE

    def rest_parts(shape):
        row = iota2(shape)[0]
        return row % beams, row // (beams * REST), row // beams % REST

    full_ref[...] = spread_weights(coefs, TILE, full_parts, full_ref.shape)
    rest_ref[...] = spread_weights(coefs, REST, rest_parts, rest_ref.shape)


def fold_weights(offsets_y, offsets_x, beams):
    rows, columns = 2 * beams[1].shape[1], 4 * HALF
    shapes = [(rows * size, columns * size) for size in (TILE, REST)]
    return pl.pallas_call(
        weights_kernel,
        in_specs=[pl.BlockSpec(memory_space=pltpu.SMEM)] * 2 + [pl.BlockSpec(memory_space=pltpu.VMEM)] * 3,
        out_specs=[pl.BlockSpec(memory_space=pltpu.VMEM)] * 2,
        out_shape=[jax.ShapeDtypeStruct(shape, jnp.bfloat16) for shape in shapes],
        compiler_params=pltpu.CompilerParams(vmem_limit_bytes=LIMIT),
        cost_estimate=pl.CostEstimate(flops=100000000, bytes_accessed=1000000, transcendentals=0),
    )(offsets_y, offsets_x, *beams)


PLACED = [(FULL, 2 * HALF * TILE, FIELD_X), (2 * HALF * REST, FIELD_X)]


def place(side, ox_ref, received_ref, full_ref, rest_ref):
    blank = jnp.zeros((2 * BAND, FIELD_X - WIN), jnp.float32)
    tails = []
    for n in range(HALF):
        shift = ox_ref[side_position(side, n)]
        both = jnp.concatenate([received_ref[n, : 2 * BAND, :], blank], axis=1)
        both = pltpu.roll(both, shift, 1)
        planes = [both[:BAND], both[BAND:]]
        for t in range(FULL):
            rows = slice(t * TILE, (t + 1) * TILE)
            pair = jnp.concatenate([planes[0][rows], planes[1][rows]], axis=0)
            full_ref[t, n * 2 * TILE : (n + 1) * 2 * TILE, :] = pair.astype(jnp.bfloat16)
        tails += [plane[FULL * TILE :] for plane in planes]
    rest_ref[...] = jnp.concatenate(tails, axis=0).astype(jnp.bfloat16)


def place_kernel(ox_ref, received_ref, full_ref, rest_ref):
    place(0, ox_ref, received_ref, full_ref, rest_ref)


def place_own(offsets_x, received):
    return pl.pallas_call(
        place_kernel,
        in_specs=[pl.BlockSpec(memory_space=pltpu.SMEM), pl.BlockSpec(memory_space=pltpu.VMEM)],
        out_specs=[pl.BlockSpec(memory_space=pltpu.VMEM)] * 2,
        out_shape=[jax.ShapeDtypeStruct(shape, jnp.bfloat16) for shape in PLACED],
        compiler_params=pltpu.CompilerParams(vmem_limit_bytes=LIMIT),
        cost_estimate=pl.CostEstimate(flops=1000000, bytes_accessed=1000000, transcendentals=0),
    )(offsets_x, received)


CHUNKS = 4


def fold_kernel(
    ox_ref, weight_ref, weight_rest_ref, own_ref, own_rest_ref, other_ref,
    out_hbm,
    full_ref, rest_ref, line_ref, sem,
):
    place(1, ox_ref, other_ref, full_ref, rest_ref)
    beams = weight_ref.shape[0] // (2 * TILE)
    length = BAND * LINES
    columns = [slice(side * WIN, (side + 1) * WIN) for side in range(FIELD_X // WIN)]

    half = own_rest_ref.shape[0]
    part = dot(weight_rest_ref[:, :half], own_rest_ref[...])
    part += dot(weight_rest_ref[:, half:], rest_ref[...])
    for group in range(2 * REST):
        plane, y = divmod(group, REST)
        value = part[group * beams : (group + 1) * beams]
        for side, column in enumerate(columns):
            start = (FULL * TILE + y) * LINES + 2 * side + plane
            line_ref[pl.ds(start, beams, stride=length), :] = value[:, column]

    half = own_ref.shape[1]
    rows, lines = weight_ref.shape[0] // CHUNKS, beams * length // CHUNKS
    copies = []
    for chunk in range(CHUNKS):
        for t in range(FULL):
            at = slice(chunk * rows, (chunk + 1) * rows)
            part = dot(weight_ref[at, :half], own_ref[t]) + dot(weight_ref[at, half:], full_ref[t])
            for group in range(rows // TILE):
                beam, plane = divmod(group, 2)
                value = part[group * TILE : (group + 1) * TILE]
                for side, column in enumerate(columns):
                    start = chunk * lines + beam * length + t * TILE * LINES + 2 * side + plane
                    line_ref[pl.ds(start, TILE, stride=LINES), :] = value[:, column]
        at = pl.ds(chunk * lines, lines)
        copy = pltpu.make_async_copy(line_ref.at[at], out_hbm.at[at], sem.at[chunk])
        copy.start()
        copies.append(copy)
    for copy in copies:
        copy.wait()


def fold(offsets_x, weights, own, other):
    lines = weights[0].shape[0] // (2 * TILE) * BAND * LINES
    operands = (*weights, *own, other)
    return pl.pallas_call(
        fold_kernel,
        in_specs=[pl.BlockSpec(memory_space=pltpu.SMEM)] + [pl.BlockSpec(memory_space=pltpu.VMEM)] * len(operands),
        out_specs=pl.BlockSpec(memory_space=pl.ANY),
        out_shape=jax.ShapeDtypeStruct((lines, WIN), jnp.float32),
        scratch_shapes=[
            *[pltpu.VMEM(shape, jnp.bfloat16) for shape in PLACED],
            pltpu.VMEM((lines, WIN), jnp.float32),
            pltpu.SemaphoreType.DMA((CHUNKS,)),
        ],
        compiler_params=pltpu.CompilerParams(vmem_limit_bytes=LIMIT),
    )(offsets_x, *operands)


def swap(value, axis, pairs):
    both = [(a, b) for a, b in pairs] + [(b, a) for a, b in pairs]
    return lax.ppermute(value, axis, both)


def body(s_matrix, beam_index, amplitude, phase, offsets_y, offsets_x, measured):
    beams_here = s_matrix.shape[0]
    depth = lax.axis_size("z")
    beams = (beam_index.T, amplitude[None, :], phase[None, :])
    s_flat = s_matrix.reshape(beams_here * 2, FIELD_Y, FIELD_X)

    keep, send = own_waves(s_flat, offsets_y, offsets_x, beams)
    pair = keep + swap(send, "core", [(0, 1)])
    total = pair[0] + swap(pair[1], "yl", [(0, 1)])
    weights = fold_weights(offsets_y, offsets_x, beams)
    for bit in (1, 2):
        other = swap(total, "z", [(i, i ^ bit) for i in range(depth) if not i & bit])
        if bit == 1:
            other, weights = lax.optimization_barrier((other, weights))
        total = total + other
    total = total + swap(total, "z", [(i, depth - 1 - i) for i in range(depth // 2)])

    copies = lax.axis_size("yl")
    blocks = misfit_blocks(offsets_y, total, measured, jnp.asarray(transform_tables()), copies)
    blocks = blocks.reshape(BANDS * copies, BLOCK, WIN)
    received = lax.all_to_all(blocks, ("pos", "yl"), 0, 0, tiled=True)
    other = swap(received, "core", [(0, 1)])
    own = place_own(offsets_x, received)
    lines = fold(offsets_x, weights, own, other)
    gradient = lines.reshape(beams_here, BAND, FIELD_X // WIN, 2, WIN).transpose(0, 3, 1, 2, 4)
    return gradient.reshape(beams_here, 2, BAND, FIELD_X)


def solution(mesh):
    fine = Mesh(mesh.devices.reshape(8, 8, 2, 2), ("pos", "z", "yl", "core"))
    beam = ("z", "yl", "core")
    return jax.shard_map(
        body,
        mesh=fine,
        in_specs=(
            P(beam, None, None, None),
            P(beam, None),
            P(beam),
            P(beam),
            P(),
            P(),
            P("pos", None, None),
        ),
        out_specs=P(beam, None, "pos", None),
        check_vma=False,
    )
```

```python
import math

import jax
import jax.numpy as jnp
import numpy as np
from jax import lax
from jax.experimental import pallas as pl
from jax.experimental.pallas import tpu as pltpu
from jax.sharding import Mesh
from jax.sharding import PartitionSpec as P

WIN = 128
FIELD_Y = 144
FIELD_X = 256
BANDS = 8
BAND = FIELD_Y // BANDS
BLOCK = 40
ROWS = 16
LIMIT = 48 * 1024 * 1024
WHOLE = 60 * 1024 * 1024


def beam_weights(rows_y, cols_x, beams):
    wave_y, wave_x, amplitude, phase = beams
    cells = FIELD_Y * FIELD_X
    count = rows_y * wave_y * FIELD_X + cols_x * wave_x * FIELD_Y
    whole = jnp.floor(count.astype(jnp.float32) * (1.0 / cells)).astype(jnp.int32)
    turns = count - whole * cells
    turns = jnp.where(turns < 0, turns + cells, turns)
    turns = jnp.where(turns >= cells, turns - cells, turns)
    angles = phase - 2.0 * math.pi / cells * turns.astype(jnp.float32)
    return amplitude * jnp.cos(angles), amplitude * jnp.sin(angles)


def places(count, offset_of, shape):
    row = lax.broadcasted_iota(jnp.int32, shape, 0)
    value = jnp.zeros(shape, jnp.int32)
    for n in range(count):
        value = jnp.where(row == n, offset_of(n), value)
    return value


def one_hot(condition):
    return jnp.where(condition, 1.0, 0.0).astype(jnp.bfloat16)


def iota2(shape):
    return [lax.broadcasted_iota(jnp.int32, shape, axis) for axis in range(2)]


def dot(left, right):
    return jnp.dot(left, right, preferred_element_type=jnp.float32)


def transform_tables():
    counter = np.arange(WIN)
    angles = 2.0 * np.pi / WIN * np.mod(counter[:, None] * counter[None, :], WIN)
    cos_table, sin_table = np.cos(angles) / math.sqrt(WIN), np.sin(angles) / math.sqrt(WIN)
    table = np.block([[cos_table, -sin_table], [sin_table, cos_table]]).astype(np.float32)
    pair = np.stack([table, table.T])
    high = pair.astype(jnp.bfloat16)
    low = (pair - high.astype(np.float32)).astype(jnp.bfloat16)
    return np.stack([high, low], axis=1)


def slot_position(slot):
    core = lax.axis_index("core") ^ (slot // 2)
    lane = lax.axis_index("yl") ^ (slot % 2)
    return lax.axis_index("pos") * 4 + 2 * core + lane


PIECE = 16
FIRST = 4


def waves_kernel(
    oy_hbm, ox_hbm, index_hbm, amplitude_hbm, phase_hbm, s_hbm,
    keep_ref, send_ref,
    oy_ref, ox_ref, index_ref, amplitude_ref, phase_ref, s_ref, mix_ref, full_ref, part_ref, small_sem, piece_sem,
):
    depth, tiles = s_ref.shape[0], FIELD_Y // ROWS
    beams = depth // 2
    small = [
        pltpu.make_async_copy(source, target, small_sem.at[i])
        for i, (source, target) in enumerate(
            [
                (oy_hbm, oy_ref),
                (ox_hbm, ox_ref),
                (index_hbm, index_ref),
                (amplitude_hbm, amplitude_ref),
                (phase_hbm, phase_ref),
            ]
        )
    ]
    large = []
    for i in range(depth // PIECE):
        planes = pl.ds(i * PIECE, PIECE)
        large.append(pltpu.make_async_copy(s_hbm.at[planes], s_ref.at[planes], piece_sem.at[i]))
    for copy in small + large[:FIRST]:
        copy.start()
    for copy in large[FIRST:]:
        copy.start(priority=1)

    outs, wide = 8, depth * ROWS
    source, column = iota2((beams, wide))
    same = source == column // (2 * ROWS)
    first = column % (2 * ROWS) < ROWS
    picks = [one_hot(same & first), one_hot(same & ~first)]
    for copy in small:
        copy.wait()
    slots = [slot_position(slot) for slot in range(4)]
    shape = (outs, beams)
    rows_y = places(outs, lambda n: oy_ref[slots[n // 2]], shape)
    cols_x = places(outs, lambda n: ox_ref[slots[n // 2]], shape)
    waves = [index_ref[0:1], index_ref[1:2], amplitude_ref[...], phase_ref[...]]
    real, imag = beam_weights(rows_y, cols_x, waves)
    is_real = iota2(shape)[0] % 2 == 0
    spread = jnp.zeros((outs * ROWS, wide), jnp.float32)
    for coef, pick in zip(
        (jnp.where(is_real, real, imag), jnp.where(is_real, -imag, real)), picks, strict=True
    ):
        tall = jnp.broadcast_to(coef[:, None, :], (outs, ROWS, beams)).reshape(outs * ROWS, beams)
        spread += dot(tall.astype(jnp.bfloat16), pick)
    row = lax.broadcasted_iota(jnp.int32, (outs * ROWS, 1), 0)
    moved = row
    for slot in range(4):
        moved += jnp.where(row // (2 * ROWS) == slot, oy_ref[slots[slot]], 0)
    column = iota2((outs * ROWS, wide))[1]
    mix_ref[...] = jnp.where(moved % ROWS == column % ROWS, spread, 0.0).astype(jnp.bfloat16)

    lefts = [lax.rem(FIELD_X - ox_ref[slots[slot]], FIELD_X) for slot in range(4)]

    def multiply(i, low, high):
        tile = s_ref[low:high, i * ROWS : (i + 1) * ROWS, :].reshape((high - low) * ROWS, FIELD_X)
        return dot(mix_ref[:, low * ROWS : high * ROWS], tile)

    def crop_columns(i):
        for slot in range(4):
            both = full_ref[i, 2 * slot * ROWS : 2 * (slot + 1) * ROWS]
            part_ref[slot, i] = pltpu.roll(both, lefts[slot], 1)[:, :WIN]

    def crop_rows(u):
        for slot in range(4):
            offset = oy_ref[slots[slot]]
            skip, rest = offset // ROWS, ROWS - offset % ROWS
            upper = iota2((2 * ROWS, WIN))[0] % ROWS < rest
            after = jnp.minimum(u + skip + 1, tiles - 1)
            value = jnp.where(upper, part_ref[slot, u + skip], part_ref[slot, after])
            ref = (keep_ref, send_ref)[slot // 2]
            for plane in range(2):
                rows = slice(u * ROWS, (u + 1) * ROWS)
                ref[slot % 2, plane, rows] = value[plane * ROWS : (plane + 1) * ROWS]

    middle = FIRST * PIECE
    for copy in large[:FIRST]:
        copy.wait()
    for i in range(tiles):
        full_ref[i] = multiply(i, 0, middle)
    for copy in large[FIRST:]:
        copy.wait()
    for i in range(tiles):
        full_ref[i] += multiply(i, middle, depth)
        crop_columns(i)
        if i >= 2:
            crop_rows(i - 2)
    crop_rows(tiles - 2)


def own_waves(s_flat, offsets_y, offsets_x, beams):
    depth = s_flat.shape[0]
    half = pltpu.VMEM((2, 2, WIN, WIN), jnp.float32)
    small = (offsets_y, offsets_x, *beams)
    operands = (*small, s_flat)
    return pl.pallas_call(
        waves_kernel,
        in_specs=[pl.BlockSpec(memory_space=pl.ANY)] * len(operands),
        out_specs=[pl.BlockSpec(memory_space=pltpu.VMEM)] * 2,
        out_shape=[half, half],
        scratch_shapes=[
            pltpu.SMEM(offsets_y.shape, jnp.int32),
            pltpu.SMEM(offsets_x.shape, jnp.int32),
            *[pltpu.VMEM(array.shape, array.dtype) for array in beams],
            pltpu.VMEM(s_flat.shape, s_flat.dtype),
            pltpu.VMEM((8 * ROWS, depth * ROWS), jnp.bfloat16),
            pltpu.VMEM((FIELD_Y // ROWS, 8 * ROWS, FIELD_X), jnp.float32),
            pltpu.VMEM((4, FIELD_Y // ROWS, 2 * ROWS, WIN), jnp.float32),
            pltpu.SemaphoreType.DMA((len(small),)),
            pltpu.SemaphoreType.DMA((depth // PIECE,)),
        ],
        compiler_params=pltpu.CompilerParams(vmem_limit_bytes=WHOLE),
    )(*operands)


def split(value):
    high = value.astype(jnp.bfloat16)
    return high, (value - high.astype(jnp.float32)).astype(jnp.bfloat16)


def product(left, right):
    return dot(left[0], right[0]) + (dot(left[1], right[0]) + dot(left[0], right[1]))


def misfit_kernel(oy_ref, wave_ref, measured_ref, table_ref, out_ref, field_ref):
    forward = (table_ref[0, 0], table_ref[0, 1])
    inverse = (table_ref[1, 0], table_ref[1, 1])

    def side(value):
        return jnp.concatenate([value[:WIN], value[WIN:]], axis=1)

    def stack(value):
        return jnp.concatenate([value[:, :WIN], value[:, WIN:]], axis=0)

    wave = jnp.concatenate([wave_ref[0], wave_ref[1]], axis=1)
    far = product(inverse, split(stack(product(split(wave), forward))))
    far_real, far_imag = far[:WIN], far[WIN:]
    modulus = jnp.sqrt(far_real * far_real + far_imag * far_imag)
    factor = 1.0 - measured_ref[lax.rem(slot_position(0), 4)] / jnp.maximum(modulus, 0.5)
    resid = jnp.concatenate([far_real * factor, far_imag * factor], axis=0)
    back = product(split(side(product(forward, split(resid)))), inverse)
    back = jnp.concatenate([back, jnp.zeros((FIELD_Y - WIN, 2 * WIN), jnp.float32)], axis=0)
    back = pltpu.roll(back, oy_ref[slot_position(0)], 0)
    for plane in range(2):
        field_ref[plane] = back[:, plane * WIN : (plane + 1) * WIN]
    copies = out_ref.shape[1]
    zeros = jnp.zeros((BLOCK - 2 * BAND, WIN), jnp.float32)
    for band in range(BANDS):
        rows = slice(band * BAND, (band + 1) * BAND)
        block = jnp.concatenate([field_ref[0, rows], field_ref[1, rows], zeros], axis=0)
        for copy in range(copies):
            out_ref[band, copy] = block


def misfit_blocks(offsets_y, wave, measured, tables, copies):
    return pl.pallas_call(
        misfit_kernel,
        in_specs=[pl.BlockSpec(memory_space=pltpu.SMEM)] + [pl.BlockSpec(memory_space=pltpu.VMEM)] * 3,
        out_specs=pl.BlockSpec(memory_space=pltpu.VMEM),
        scratch_shapes=[pltpu.VMEM((2, FIELD_Y, WIN), jnp.float32)],
        out_shape=jax.ShapeDtypeStruct((BANDS, copies, BLOCK, WIN), jnp.float32),
        compiler_params=pltpu.CompilerParams(vmem_limit_bytes=LIMIT),
    )(offsets_y, wave, measured, tables)


TILE = 8
FULL = BAND // TILE
REST = BAND - FULL * TILE
HALF = 16
LINES = 2 * FIELD_X // WIN


def side_position(side, n):
    core = lax.axis_index("core") ^ side
    return n // 2 * 4 + 2 * core + n % 2


def spread_weights(coefs, size, row_parts, shape):
    count, beams = coefs[0].shape
    beam, plane, _ = row_parts((shape[0], beams))
    pick = one_hot(beam == iota2((shape[0], beams))[1])
    real, imag = [
        lax.dot_general(pick, coef, (((1,), (1,)), ((), ())), preferred_element_type=jnp.float32)
        for coef in coefs
    ]
    first = row_parts((shape[0], count))[1] == 0
    source, column = iota2((count, shape[1]))
    same = source == column // (2 * size)
    low = column % (2 * size) < size
    spread = dot(jnp.where(first, real, -imag).astype(jnp.bfloat16), one_hot(same & low))
    spread += dot(jnp.where(first, imag, real).astype(jnp.bfloat16), one_hot(same & ~low))
    equal = row_parts(shape)[2] == iota2(shape)[1] % size
    return jnp.where(equal, spread, 0.0).astype(jnp.bfloat16)


def weights_kernel(oy_ref, ox_ref, index_ref, amplitude_ref, phase_ref, full_ref, rest_ref):
    beams, count = index_ref.shape[1], 2 * HALF
    where = [side_position(n // HALF, n % HALF) for n in range(count)]
    shape = (count, beams)
    rows_y = places(count, lambda n: oy_ref[where[n]], shape)
    cols_x = places(count, lambda n: ox_ref[where[n]], shape)
    waves = [index_ref[0:1], index_ref[1:2], amplitude_ref[...], phase_ref[...]]
    coefs = [value.astype(jnp.bfloat16) for value in beam_weights(rows_y, cols_x, waves)]

    def full_parts(shape):
        row = iota2(shape)[0]
        return row // (2 * TILE), row // TILE % 2, row % TILE

    def rest_parts(shape):
        row = iota2(shape)[0]
        return row % beams, row // (beams * REST), row // beams % REST

    full_ref[...] = spread_weights(coefs, TILE, full_parts, full_ref.shape)
    rest_ref[...] = spread_weights(coefs, REST, rest_parts, rest_ref.shape)


def fold_weights(offsets_y, offsets_x, beams):
    rows, columns = 2 * beams[1].shape[1], 4 * HALF
    shapes = [(rows * size, columns * size) for size in (TILE, REST)]
    return pl.pallas_call(
        weights_kernel,
        in_specs=[pl.BlockSpec(memory_space=pltpu.SMEM)] * 2 + [pl.BlockSpec(memory_space=pltpu.VMEM)] * 3,
        out_specs=[pl.BlockSpec(memory_space=pltpu.VMEM)] * 2,
        out_shape=[jax.ShapeDtypeStruct(shape, jnp.bfloat16) for shape in shapes],
        compiler_params=pltpu.CompilerParams(vmem_limit_bytes=LIMIT),
        cost_estimate=pl.CostEstimate(flops=100000000, bytes_accessed=1000000, transcendentals=0),
    )(offsets_y, offsets_x, *beams)


PLACED = [(FULL, 2 * HALF * TILE, FIELD_X), (2 * HALF * REST, FIELD_X)]


def place(side, ox_ref, received_ref, full_ref, rest_ref):
    blank = jnp.zeros((2 * BAND, FIELD_X - WIN), jnp.float32)
    tails = []
    for n in range(HALF):
        shift = ox_ref[side_position(side, n)]
        both = jnp.concatenate([received_ref[n, : 2 * BAND, :], blank], axis=1)
        both = pltpu.roll(both, shift, 1)
        planes = [both[:BAND], both[BAND:]]
        for t in range(FULL):
            rows = slice(t * TILE, (t + 1) * TILE)
            pair = jnp.concatenate([planes[0][rows], planes[1][rows]], axis=0)
            full_ref[t, n * 2 * TILE : (n + 1) * 2 * TILE, :] = pair.astype(jnp.bfloat16)
        tails += [plane[FULL * TILE :] for plane in planes]
    rest_ref[...] = jnp.concatenate(tails, axis=0).astype(jnp.bfloat16)


def place_kernel(ox_ref, received_ref, full_ref, rest_ref):
    place(0, ox_ref, received_ref, full_ref, rest_ref)


def place_own(offsets_x, received):
    return pl.pallas_call(
        place_kernel,
        in_specs=[pl.BlockSpec(memory_space=pltpu.SMEM), pl.BlockSpec(memory_space=pltpu.VMEM)],
        out_specs=[pl.BlockSpec(memory_space=pltpu.VMEM)] * 2,
        out_shape=[jax.ShapeDtypeStruct(shape, jnp.bfloat16) for shape in PLACED],
        compiler_params=pltpu.CompilerParams(vmem_limit_bytes=LIMIT),
        cost_estimate=pl.CostEstimate(flops=1000000, bytes_accessed=1000000, transcendentals=0),
    )(offsets_x, received)


CHUNKS = 4


def fold_kernel(
    ox_ref, weight_ref, weight_rest_ref, own_ref, own_rest_ref, other_ref,
    out_hbm,
    full_ref, rest_ref, line_ref, sem,
):
    place(1, ox_ref, other_ref, full_ref, rest_ref)
    beams = weight_ref.shape[0] // (2 * TILE)
    length = BAND * LINES
    columns = [slice(side * WIN, (side + 1) * WIN) for side in range(FIELD_X // WIN)]

    half = own_rest_ref.shape[0]
    part = dot(weight_rest_ref[:, :half], own_rest_ref[...])
    part += dot(weight_rest_ref[:, half:], rest_ref[...])
    for group in range(2 * REST):
        plane, y = divmod(group, REST)
        value = part[group * beams : (group + 1) * beams]
        for side, column in enumerate(columns):
            start = (FULL * TILE + y) * LINES + 2 * side + plane
            line_ref[pl.ds(start, beams, stride=length), :] = value[:, column]

    half = own_ref.shape[1]
    rows, lines = weight_ref.shape[0] // CHUNKS, beams * length // CHUNKS
    copies = []
    for chunk in range(CHUNKS):
        for t in range(FULL):
            at = slice(chunk * rows, (chunk + 1) * rows)
            part = dot(weight_ref[at, :half], own_ref[t]) + dot(weight_ref[at, half:], full_ref[t])
            for group in range(rows // TILE):
                beam, plane = divmod(group, 2)
                value = part[group * TILE : (group + 1) * TILE]
                for side, column in enumerate(columns):
                    start = chunk * lines + beam * length + t * TILE * LINES + 2 * side + plane
                    line_ref[pl.ds(start, TILE, stride=LINES), :] = value[:, column]
        at = pl.ds(chunk * lines, lines)
        copy = pltpu.make_async_copy(line_ref.at[at], out_hbm.at[at], sem.at[chunk])
        copy.start()
        copies.append(copy)
    for copy in copies:
        copy.wait()


def fold(offsets_x, weights, own, other):
    lines = weights[0].shape[0] // (2 * TILE) * BAND * LINES
    operands = (*weights, *own, other)
    return pl.pallas_call(
        fold_kernel,
        in_specs=[pl.BlockSpec(memory_space=pltpu.SMEM)] + [pl.BlockSpec(memory_space=pltpu.VMEM)] * len(operands),
        out_specs=pl.BlockSpec(memory_space=pl.ANY),
        out_shape=jax.ShapeDtypeStruct((lines, WIN), jnp.float32),
        scratch_shapes=[
            *[pltpu.VMEM(shape, jnp.bfloat16) for shape in PLACED],
            pltpu.VMEM((lines + BAND * LINES, WIN), jnp.float32),
            pltpu.SemaphoreType.DMA((CHUNKS,)),
        ],
        compiler_params=pltpu.CompilerParams(vmem_limit_bytes=LIMIT),
    )(offsets_x, *operands)


def swap(value, axis, pairs):
    both = [(a, b) for a, b in pairs] + [(b, a) for a, b in pairs]
    return lax.ppermute(value, axis, both)


def body(s_matrix, beam_index, amplitude, phase, offsets_y, offsets_x, measured):
    beams_here = s_matrix.shape[0]
    depth = lax.axis_size("z")
    beams = (beam_index.T, amplitude[None, :], phase[None, :])
    s_flat = s_matrix.reshape(beams_here * 2, FIELD_Y, FIELD_X)

    keep, send = own_waves(s_flat, offsets_y, offsets_x, beams)
    pair = keep + swap(send, "core", [(0, 1)])
    total = pair[0] + swap(pair[1], "yl", [(0, 1)])
    weights = fold_weights(offsets_y, offsets_x, beams)
    for bit in (1, 2):
        other = swap(total, "z", [(i, i ^ bit) for i in range(depth) if not i & bit])
        if bit == 1:
            other, weights = lax.optimization_barrier((other, weights))
        total = total + other
    total = total + swap(total, "z", [(i, depth - 1 - i) for i in range(depth // 2)])

    copies = lax.axis_size("yl")
    blocks = misfit_blocks(offsets_y, total, measured, jnp.asarray(transform_tables()), copies)
    blocks = blocks.reshape(BANDS * copies, BLOCK, WIN)
    received = lax.all_to_all(blocks, ("pos", "yl"), 0, 0, tiled=True)
    other = swap(received, "core", [(0, 1)])
    own = place_own(offsets_x, received)
    lines = fold(offsets_x, weights, own, other)
    gradient = lines.reshape(beams_here, BAND, FIELD_X // WIN, 2, WIN).transpose(0, 3, 1, 2, 4)
    return gradient.reshape(beams_here, 2, BAND, FIELD_X)


def solution(mesh):
    fine = Mesh(mesh.devices.reshape(8, 8, 2, 2), ("pos", "z", "yl", "core"))
    beam = ("z", "yl", "core")
    return jax.shard_map(
        body,
        mesh=fine,
        in_specs=(
            P(beam, None, None, None),
            P(beam, None),
            P(beam),
            P(beam),
            P(),
            P(),
            P("pos", None, None),
        ),
        out_specs=P(beam, None, "pos", None),
        check_vma=False,
    )
```

```python
import math

import jax
import jax.numpy as jnp
import numpy as np
from jax import lax
from jax.experimental import pallas as pl
from jax.experimental.pallas import tpu as pltpu
from jax.sharding import Mesh
from jax.sharding import PartitionSpec as P

WIN = 128
FIELD_Y = 144
FIELD_X = 256
BANDS = 8
BAND = FIELD_Y // BANDS
BLOCK = 40
ROWS = 16
LIMIT = 48 * 1024 * 1024
WHOLE = 60 * 1024 * 1024


def beam_weights(rows_y, cols_x, beams):
    wave_y, wave_x, amplitude, phase = beams
    cells = FIELD_Y * FIELD_X
    count = rows_y * wave_y * FIELD_X + cols_x * wave_x * FIELD_Y
    whole = jnp.floor(count.astype(jnp.float32) * (1.0 / cells)).astype(jnp.int32)
    turns = count - whole * cells
    turns = jnp.where(turns < 0, turns + cells, turns)
    turns = jnp.where(turns >= cells, turns - cells, turns)
    angles = phase - 2.0 * math.pi / cells * turns.astype(jnp.float32)
    return amplitude * jnp.cos(angles), amplitude * jnp.sin(angles)


def places(count, offset_of, shape):
    row = lax.broadcasted_iota(jnp.int32, shape, 0)
    value = jnp.zeros(shape, jnp.int32)
    for n in range(count):
        value = jnp.where(row == n, offset_of(n), value)
    return value


def one_hot(condition):
    return jnp.where(condition, 1.0, 0.0).astype(jnp.bfloat16)


def iota2(shape):
    return [lax.broadcasted_iota(jnp.int32, shape, axis) for axis in range(2)]


def dot(left, right):
    return jnp.dot(left, right, preferred_element_type=jnp.float32)


def transform_tables():
    counter = np.arange(WIN)
    angles = 2.0 * np.pi / WIN * np.mod(counter[:, None] * counter[None, :], WIN)
    cos_table, sin_table = np.cos(angles) / math.sqrt(WIN), np.sin(angles) / math.sqrt(WIN)
    table = np.block([[cos_table, -sin_table], [sin_table, cos_table]]).astype(np.float32)
    pair = np.stack([table, table.T])
    high = pair.astype(jnp.bfloat16)
    low = (pair - high.astype(np.float32)).astype(jnp.bfloat16)
    return np.stack([high, low], axis=1)


def slot_position(slot):
    core = lax.axis_index("core") ^ (slot // 2)
    lane = lax.axis_index("yl") ^ (slot % 2)
    return lax.axis_index("pos") * 4 + 2 * core + lane


PIECE = 16
STAGES = (3, 6, 8)


def waves_kernel(
    oy_hbm, ox_hbm, index_hbm, amplitude_hbm, phase_hbm, s_hbm,
    keep_ref, send_ref,
    oy_ref, ox_ref, index_ref, amplitude_ref, phase_ref, s_ref, mix_ref, full_ref, part_ref, small_sem, piece_sem,
):
    depth, tiles = s_ref.shape[0], FIELD_Y // ROWS
    beams = depth // 2
    small = [
        pltpu.make_async_copy(source, target, small_sem.at[i])
        for i, (source, target) in enumerate(
            [
                (oy_hbm, oy_ref),
                (ox_hbm, ox_ref),
                (index_hbm, index_ref),
                (amplitude_hbm, amplitude_ref),
                (phase_hbm, phase_ref),
            ]
        )
    ]
    large = []
    for i in range(depth // PIECE):
        planes = pl.ds(i * PIECE, PIECE)
        large.append(pltpu.make_async_copy(s_hbm.at[planes], s_ref.at[planes], piece_sem.at[i]))
    for copy in small + large[: STAGES[0]]:
        copy.start()
    for copy in large[STAGES[0] :]:
        copy.start(priority=1)

    outs, wide = 8, depth * ROWS
    source, column = iota2((beams, wide))
    same = source == column // (2 * ROWS)
    first = column % (2 * ROWS) < ROWS
    picks = [one_hot(same & first), one_hot(same & ~first)]
    for copy in small:
        copy.wait()
    slots = [slot_position(slot) for slot in range(4)]
    shape = (outs, beams)
    rows_y = places(outs, lambda n: oy_ref[slots[n // 2]], shape)
    cols_x = places(outs, lambda n: ox_ref[slots[n // 2]], shape)
    waves = [index_ref[0:1], index_ref[1:2], amplitude_ref[...], phase_ref[...]]
    real, imag = beam_weights(rows_y, cols_x, waves)
    is_real = iota2(shape)[0] % 2 == 0
    spread = jnp.zeros((outs * ROWS, wide), jnp.float32)
    for coef, pick in zip(
        (jnp.where(is_real, real, imag), jnp.where(is_real, -imag, real)), picks, strict=True
    ):
        tall = jnp.broadcast_to(coef[:, None, :], (outs, ROWS, beams)).reshape(outs * ROWS, beams)
        spread += dot(tall.astype(jnp.bfloat16), pick)
    row = lax.broadcasted_iota(jnp.int32, (outs * ROWS, 1), 0)
    moved = row
    for slot in range(4):
        moved += jnp.where(row // (2 * ROWS) == slot, oy_ref[slots[slot]], 0)
    column = iota2((outs * ROWS, wide))[1]
    mix_ref[...] = jnp.where(moved % ROWS == column % ROWS, spread, 0.0).astype(jnp.bfloat16)

    lefts = [lax.rem(FIELD_X - ox_ref[slots[slot]], FIELD_X) for slot in range(4)]

    def multiply(i, low, high):
        low, high = low * PIECE, high * PIECE
        tile = s_ref[low:high, i * ROWS : (i + 1) * ROWS, :].reshape((high - low) * ROWS, FIELD_X)
        return dot(mix_ref[:, low * ROWS : high * ROWS], tile)

    def crop_columns(i):
        for slot in range(4):
            both = full_ref[i, 2 * slot * ROWS : 2 * (slot + 1) * ROWS]
            part_ref[slot, i] = pltpu.roll(both, lefts[slot], 1)[:, :WIN]

    def crop_rows(u):
        for slot in range(4):
            offset = oy_ref[slots[slot]]
            skip, rest = offset // ROWS, ROWS - offset % ROWS
            upper = iota2((2 * ROWS, WIN))[0] % ROWS < rest
            after = jnp.minimum(u + skip + 1, tiles - 1)
            value = jnp.where(upper, part_ref[slot, u + skip], part_ref[slot, after])
            ref = (keep_ref, send_ref)[slot // 2]
            for plane in range(2):
                rows = slice(u * ROWS, (u + 1) * ROWS)
                ref[slot % 2, plane, rows] = value[plane * ROWS : (plane + 1) * ROWS]

    for low, high in zip((0, *STAGES), STAGES):
        for copy in large[low:high]:
            copy.wait()
        for i in range(tiles):
            part = multiply(i, low, high)
            full_ref[i] = full_ref[i] + part if low else part
            if high == len(large):
                crop_columns(i)
                if i >= 2:
                    crop_rows(i - 2)
    crop_rows(tiles - 2)


def own_waves(s_flat, offsets_y, offsets_x, beams):
    depth = s_flat.shape[0]
    half = pltpu.VMEM((2, 2, WIN, WIN), jnp.float32)
    small = (offsets_y, offsets_x, *beams)
    operands = (*small, s_flat)
    return pl.pallas_call(
        waves_kernel,
        in_specs=[pl.BlockSpec(memory_space=pl.ANY)] * len(operands),
        out_specs=[pl.BlockSpec(memory_space=pltpu.VMEM)] * 2,
        out_shape=[half, half],
        scratch_shapes=[
            pltpu.SMEM(offsets_y.shape, jnp.int32),
            pltpu.SMEM(offsets_x.shape, jnp.int32),
            *[pltpu.VMEM(array.shape, array.dtype) for array in beams],
            pltpu.VMEM(s_flat.shape, s_flat.dtype),
            pltpu.VMEM((8 * ROWS, depth * ROWS), jnp.bfloat16),
            pltpu.VMEM((FIELD_Y // ROWS, 8 * ROWS, FIELD_X), jnp.float32),
            pltpu.VMEM((4, FIELD_Y // ROWS, 2 * ROWS, WIN), jnp.float32),
            pltpu.SemaphoreType.DMA((len(small),)),
            pltpu.SemaphoreType.DMA((depth // PIECE,)),
        ],
        compiler_params=pltpu.CompilerParams(vmem_limit_bytes=WHOLE),
    )(*operands)


def split(value):
    high = value.astype(jnp.bfloat16)
    return high, (value - high.astype(jnp.float32)).astype(jnp.bfloat16)


def product(left, right):
    return dot(left[0], right[0]) + (dot(left[1], right[0]) + dot(left[0], right[1]))


def misfit_kernel(oy_ref, wave_ref, measured_ref, table_ref, out_ref, field_ref):
    forward = (table_ref[0, 0], table_ref[0, 1])
    inverse = (table_ref[1, 0], table_ref[1, 1])

    def side(value):
        return jnp.concatenate([value[:WIN], value[WIN:]], axis=1)

    def stack(value):
        return jnp.concatenate([value[:, :WIN], value[:, WIN:]], axis=0)

    wave = jnp.concatenate([wave_ref[0], wave_ref[1]], axis=1)
    far = product(inverse, split(stack(product(split(wave), forward))))
    far_real, far_imag = far[:WIN], far[WIN:]
    modulus = jnp.sqrt(far_real * far_real + far_imag * far_imag)
    factor = 1.0 - measured_ref[lax.rem(slot_position(0), 4)] / jnp.maximum(modulus, 0.5)
    resid = jnp.concatenate([far_real * factor, far_imag * factor], axis=0)
    back = product(split(side(product(forward, split(resid)))), inverse)
    back = jnp.concatenate([back, jnp.zeros((FIELD_Y - WIN, 2 * WIN), jnp.float32)], axis=0)
    back = pltpu.roll(back, oy_ref[slot_position(0)], 0)
    for plane in range(2):
        field_ref[plane] = back[:, plane * WIN : (plane + 1) * WIN]
    copies = out_ref.shape[1]
    zeros = jnp.zeros((BLOCK - 2 * BAND, WIN), jnp.float32)
    for band in range(BANDS):
        rows = slice(band * BAND, (band + 1) * BAND)
        block = jnp.concatenate([field_ref[0, rows], field_ref[1, rows], zeros], axis=0)
        for copy in range(copies):
            out_ref[band, copy] = block


def misfit_blocks(offsets_y, wave, measured, tables, copies):
    return pl.pallas_call(
        misfit_kernel,
        in_specs=[pl.BlockSpec(memory_space=pltpu.SMEM)] + [pl.BlockSpec(memory_space=pltpu.VMEM)] * 3,
        out_specs=pl.BlockSpec(memory_space=pltpu.VMEM),
        scratch_shapes=[pltpu.VMEM((2, FIELD_Y, WIN), jnp.float32)],
        out_shape=jax.ShapeDtypeStruct((BANDS, copies, BLOCK, WIN), jnp.float32),
        compiler_params=pltpu.CompilerParams(vmem_limit_bytes=LIMIT),
    )(offsets_y, wave, measured, tables)


TILE = 8
FULL = BAND // TILE
REST = BAND - FULL * TILE
HALF = 16
LINES = 2 * FIELD_X // WIN


def side_position(side, n):
    core = lax.axis_index("core") ^ side
    return n // 2 * 4 + 2 * core + n % 2


def spread_weights(coefs, size, row_parts, shape):
    count, beams = coefs[0].shape
    beam, plane, _ = row_parts((shape[0], beams))
    pick = one_hot(beam == iota2((shape[0], beams))[1])
    real, imag = [
        lax.dot_general(pick, coef, (((1,), (1,)), ((), ())), preferred_element_type=jnp.float32)
        for coef in coefs
    ]
    first = row_parts((shape[0], count))[1] == 0
    source, column = iota2((count, shape[1]))
    same = source == column // (2 * size)
    low = column % (2 * size) < size
    spread = dot(jnp.where(first, real, -imag).astype(jnp.bfloat16), one_hot(same & low))
    spread += dot(jnp.where(first, imag, real).astype(jnp.bfloat16), one_hot(same & ~low))
    equal = row_parts(shape)[2] == iota2(shape)[1] % size
    return jnp.where(equal, spread, 0.0).astype(jnp.bfloat16)


def weights_kernel(oy_ref, ox_ref, index_ref, amplitude_ref, phase_ref, full_ref, rest_ref):
    beams, count = index_ref.shape[1], 2 * HALF
    where = [side_position(n // HALF, n % HALF) for n in range(count)]
    shape = (count, beams)
    rows_y = places(count, lambda n: oy_ref[where[n]], shape)
    cols_x = places(count, lambda n: ox_ref[where[n]], shape)
    waves = [index_ref[0:1], index_ref[1:2], amplitude_ref[...], phase_ref[...]]
    coefs = [value.astype(jnp.bfloat16) for value in beam_weights(rows_y, cols_x, waves)]

    def full_parts(shape):
        row = iota2(shape)[0]
        return row // (2 * TILE), row // TILE % 2, row % TILE

    def rest_parts(shape):
        row = iota2(shape)[0]
        return row % beams, row // (beams * REST), row // beams % REST

    full_ref[...] = spread_weights(coefs, TILE, full_parts, full_ref.shape)
    rest_ref[...] = spread_weights(coefs, REST, rest_parts, rest_ref.shape)


def fold_weights(offsets_y, offsets_x, beams):
    rows, columns = 2 * beams[1].shape[1], 4 * HALF
    shapes = [(rows * size, columns * size) for size in (TILE, REST)]
    return pl.pallas_call(
        weights_kernel,
        in_specs=[pl.BlockSpec(memory_space=pltpu.SMEM)] * 2 + [pl.BlockSpec(memory_space=pltpu.VMEM)] * 3,
        out_specs=[pl.BlockSpec(memory_space=pltpu.VMEM)] * 2,
        out_shape=[jax.ShapeDtypeStruct(shape, jnp.bfloat16) for shape in shapes],
        compiler_params=pltpu.CompilerParams(vmem_limit_bytes=LIMIT),
        cost_estimate=pl.CostEstimate(flops=100000000, bytes_accessed=1000000, transcendentals=0),
    )(offsets_y, offsets_x, *beams)


PLACED = [(FULL, 2 * HALF * TILE, FIELD_X), (2 * HALF * REST, FIELD_X)]


def place(side, ox_ref, received_ref, full_ref, rest_ref):
    blank = jnp.zeros((2 * BAND, FIELD_X - WIN), jnp.float32)
    tails = []
    for n in range(HALF):
        shift = ox_ref[side_position(side, n)]
        both = jnp.concatenate([received_ref[n, : 2 * BAND, :], blank], axis=1)
        both = pltpu.roll(both, shift, 1)
        planes = [both[:BAND], both[BAND:]]
        for t in range(FULL):
            rows = slice(t * TILE, (t + 1) * TILE)
            pair = jnp.concatenate([planes[0][rows], planes[1][rows]], axis=0)
            full_ref[t, n * 2 * TILE : (n + 1) * 2 * TILE, :] = pair.astype(jnp.bfloat16)
        tails += [plane[FULL * TILE :] for plane in planes]
    rest_ref[...] = jnp.concatenate(tails, axis=0).astype(jnp.bfloat16)


def place_kernel(ox_ref, received_ref, full_ref, rest_ref):
    place(0, ox_ref, received_ref, full_ref, rest_ref)


def place_own(offsets_x, received):
    return pl.pallas_call(
        place_kernel,
        in_specs=[pl.BlockSpec(memory_space=pltpu.SMEM), pl.BlockSpec(memory_space=pltpu.VMEM)],
        out_specs=[pl.BlockSpec(memory_space=pltpu.VMEM)] * 2,
        out_shape=[jax.ShapeDtypeStruct(shape, jnp.bfloat16) for shape in PLACED],
        compiler_params=pltpu.CompilerParams(vmem_limit_bytes=LIMIT),
        cost_estimate=pl.CostEstimate(flops=1000000, bytes_accessed=1000000, transcendentals=0),
    )(offsets_x, received)


CHUNKS = 4


def fold_kernel(
    ox_ref, weight_ref, weight_rest_ref, own_ref, own_rest_ref, other_ref,
    out_hbm,
    full_ref, rest_ref, line_ref, sem,
):
    place(1, ox_ref, other_ref, full_ref, rest_ref)
    beams = weight_ref.shape[0] // (2 * TILE)
    length = BAND * LINES
    columns = [slice(side * WIN, (side + 1) * WIN) for side in range(FIELD_X // WIN)]

    half = own_rest_ref.shape[0]
    part = dot(weight_rest_ref[:, :half], own_rest_ref[...])
    part += dot(weight_rest_ref[:, half:], rest_ref[...])
    for group in range(2 * REST):
        plane, y = divmod(group, REST)
        value = part[group * beams : (group + 1) * beams]
        for side, column in enumerate(columns):
            start = (FULL * TILE + y) * LINES + 2 * side + plane
            line_ref[pl.ds(start, beams, stride=length), :] = value[:, column]

    half = own_ref.shape[1]
    rows, lines = weight_ref.shape[0] // CHUNKS, beams * length // CHUNKS
    copies = []
    for chunk in range(CHUNKS):
        for t in range(FULL):
            at = slice(chunk * rows, (chunk + 1) * rows)
            part = dot(weight_ref[at, :half], own_ref[t]) + dot(weight_ref[at, half:], full_ref[t])
            for group in range(rows // TILE):
                beam, plane = divmod(group, 2)
                value = part[group * TILE : (group + 1) * TILE]
                for side, column in enumerate(columns):
                    start = chunk * lines + beam * length + t * TILE * LINES + 2 * side + plane
                    line_ref[pl.ds(start, TILE, stride=LINES), :] = value[:, column]
        at = pl.ds(chunk * lines, lines)
        copy = pltpu.make_async_copy(line_ref.at[at], out_hbm.at[at], sem.at[chunk])
        copy.start()
        copies.append(copy)
    for copy in copies:
        copy.wait()


def fold(offsets_x, weights, own, other):
    lines = weights[0].shape[0] // (2 * TILE) * BAND * LINES
    operands = (*weights, *own, other)
    return pl.pallas_call(
        fold_kernel,
        in_specs=[pl.BlockSpec(memory_space=pltpu.SMEM)] + [pl.BlockSpec(memory_space=pltpu.VMEM)] * len(operands),
        out_specs=pl.BlockSpec(memory_space=pl.ANY),
        out_shape=jax.ShapeDtypeStruct((lines, WIN), jnp.float32),
        scratch_shapes=[
            *[pltpu.VMEM(shape, jnp.bfloat16) for shape in PLACED],
            pltpu.VMEM((lines + BAND * LINES, WIN), jnp.float32),
            pltpu.SemaphoreType.DMA((CHUNKS,)),
        ],
        compiler_params=pltpu.CompilerParams(vmem_limit_bytes=LIMIT),
    )(offsets_x, *operands)


def swap(value, axis, pairs):
    both = [(a, b) for a, b in pairs] + [(b, a) for a, b in pairs]
    return lax.ppermute(value, axis, both)


def body(s_matrix, beam_index, amplitude, phase, offsets_y, offsets_x, measured):
    beams_here = s_matrix.shape[0]
    depth = lax.axis_size("z")
    beams = (beam_index.T, amplitude[None, :], phase[None, :])
    s_flat = s_matrix.reshape(beams_here * 2, FIELD_Y, FIELD_X)

    keep, send = own_waves(s_flat, offsets_y, offsets_x, beams)
    pair = keep + swap(send, "core", [(0, 1)])
    total = pair[0] + swap(pair[1], "yl", [(0, 1)])
    weights = fold_weights(offsets_y, offsets_x, beams)
    for bit in (1, 2):
        other = swap(total, "z", [(i, i ^ bit) for i in range(depth) if not i & bit])
        if bit == 1:
            other, weights = lax.optimization_barrier((other, weights))
        total = total + other
    total = total + swap(total, "z", [(i, depth - 1 - i) for i in range(depth // 2)])

    copies = lax.axis_size("yl")
    blocks = misfit_blocks(offsets_y, total, measured, jnp.asarray(transform_tables()), copies)
    blocks = blocks.reshape(BANDS * copies, BLOCK, WIN)
    received = lax.all_to_all(blocks, ("pos", "yl"), 0, 0, tiled=True)
    other = swap(received, "core", [(0, 1)])
    own = place_own(offsets_x, received)
    lines = fold(offsets_x, weights, own, other)
    gradient = lines.reshape(beams_here, BAND, FIELD_X // WIN, 2, WIN).transpose(0, 3, 1, 2, 4)
    return gradient.reshape(beams_here, 2, BAND, FIELD_X)


def solution(mesh):
    fine = Mesh(mesh.devices.reshape(8, 8, 2, 2), ("pos", "z", "yl", "core"))
    beam = ("z", "yl", "core")
    return jax.shard_map(
        body,
        mesh=fine,
        in_specs=(
            P(beam, None, None, None),
            P(beam, None),
            P(beam),
            P(beam),
            P(),
            P(),
            P("pos", None, None),
        ),
        out_specs=P(beam, None, "pos", None),
        check_vma=False,
    )
```

```python
import math

import jax
import jax.numpy as jnp
import numpy as np
from jax import lax
from jax.experimental import pallas as pl
from jax.experimental.pallas import tpu as pltpu
from jax.sharding import Mesh
from jax.sharding import PartitionSpec as P

WIN = 128
FIELD_Y = 144
FIELD_X = 256
BANDS = 8
BAND = FIELD_Y // BANDS
BLOCK = 40
ROWS = 16
LIMIT = 48 * 1024 * 1024
WHOLE = 60 * 1024 * 1024


def beam_weights(rows_y, cols_x, beams):
    wave_y, wave_x, amplitude, phase = beams
    cells = FIELD_Y * FIELD_X
    count = rows_y * wave_y * FIELD_X + cols_x * wave_x * FIELD_Y
    whole = jnp.floor(count.astype(jnp.float32) * (1.0 / cells)).astype(jnp.int32)
    turns = count - whole * cells
    turns = jnp.where(turns < 0, turns + cells, turns)
    turns = jnp.where(turns >= cells, turns - cells, turns)
    angles = phase - 2.0 * math.pi / cells * turns.astype(jnp.float32)
    return amplitude * jnp.cos(angles), amplitude * jnp.sin(angles)


def places(count, offset_of, shape):
    row = lax.broadcasted_iota(jnp.int32, shape, 0)
    value = jnp.zeros(shape, jnp.int32)
    for n in range(count):
        value = jnp.where(row == n, offset_of(n), value)
    return value


def one_hot(condition):
    return jnp.where(condition, 1.0, 0.0).astype(jnp.bfloat16)


def iota2(shape):
    return [lax.broadcasted_iota(jnp.int32, shape, axis) for axis in range(2)]


def dot(left, right):
    return jnp.dot(left, right, preferred_element_type=jnp.float32)


def transform_tables():
    counter = np.arange(WIN)
    angles = 2.0 * np.pi / WIN * np.mod(counter[:, None] * counter[None, :], WIN)
    cos_table, sin_table = np.cos(angles) / math.sqrt(WIN), np.sin(angles) / math.sqrt(WIN)
    table = np.block([[cos_table, -sin_table], [sin_table, cos_table]]).astype(np.float32)
    pair = np.stack([table, table.T])
    high = pair.astype(jnp.bfloat16)
    low = (pair - high.astype(np.float32)).astype(jnp.bfloat16)
    return np.stack([high, low], axis=1)


def slot_position(slot):
    core = lax.axis_index("core") ^ (slot // 2)
    lane = lax.axis_index("yl") ^ (slot % 2)
    return lax.axis_index("pos") * 4 + 2 * core + lane


PIECE = 16
STAGES = (3, 6, 8)


def waves_kernel(
    oy_hbm, ox_hbm, index_hbm, amplitude_hbm, phase_hbm, s_hbm,
    slot0_ref, slot1_ref, slot2_ref, slot3_ref,
    oy_ref, ox_ref, index_ref, amplitude_ref, phase_ref, s_ref, mix_ref, full_ref, part_ref, small_sem, piece_sem,
):
    depth, tiles = s_ref.shape[0], FIELD_Y // ROWS
    beams = depth // 2
    small = [
        pltpu.make_async_copy(source, target, small_sem.at[i])
        for i, (source, target) in enumerate(
            [
                (oy_hbm, oy_ref),
                (ox_hbm, ox_ref),
                (index_hbm, index_ref),
                (amplitude_hbm, amplitude_ref),
                (phase_hbm, phase_ref),
            ]
        )
    ]
    large = []
    for i in range(depth // PIECE):
        planes = pl.ds(i * PIECE, PIECE)
        large.append(pltpu.make_async_copy(s_hbm.at[planes], s_ref.at[planes], piece_sem.at[i]))
    for copy in small + large[: STAGES[0]]:
        copy.start()
    for copy in large[STAGES[0] :]:
        copy.start(priority=1)

    outs, wide = 8, depth * ROWS
    source, column = iota2((beams, wide))
    same = source == column // (2 * ROWS)
    first = column % (2 * ROWS) < ROWS
    picks = [one_hot(same & first), one_hot(same & ~first)]
    for copy in small:
        copy.wait()
    slots = [slot_position(slot) for slot in range(4)]
    shape = (outs, beams)
    rows_y = places(outs, lambda n: oy_ref[slots[n // 2]], shape)
    cols_x = places(outs, lambda n: ox_ref[slots[n // 2]], shape)
    waves = [index_ref[0:1], index_ref[1:2], amplitude_ref[...], phase_ref[...]]
    real, imag = beam_weights(rows_y, cols_x, waves)
    is_real = iota2(shape)[0] % 2 == 0
    spread = jnp.zeros((outs * ROWS, wide), jnp.float32)
    for coef, pick in zip(
        (jnp.where(is_real, real, imag), jnp.where(is_real, -imag, real)), picks, strict=True
    ):
        tall = jnp.broadcast_to(coef[:, None, :], (outs, ROWS, beams)).reshape(outs * ROWS, beams)
        spread += dot(tall.astype(jnp.bfloat16), pick)
    row = lax.broadcasted_iota(jnp.int32, (outs * ROWS, 1), 0)
    moved = row
    for slot in range(4):
        moved += jnp.where(row // (2 * ROWS) == slot, oy_ref[slots[slot]], 0)
    column = iota2((outs * ROWS, wide))[1]
    mix_ref[...] = jnp.where(moved % ROWS == column % ROWS, spread, 0.0).astype(jnp.bfloat16)

    lefts = [lax.rem(FIELD_X - ox_ref[slots[slot]], FIELD_X) for slot in range(4)]

    def multiply(i, low, high):
        low, high = low * PIECE, high * PIECE
        tile = s_ref[low:high, i * ROWS : (i + 1) * ROWS, :].reshape((high - low) * ROWS, FIELD_X)
        return dot(mix_ref[:, low * ROWS : high * ROWS], tile)

    def crop_columns(i):
        for slot in range(4):
            both = full_ref[i, 2 * slot * ROWS : 2 * (slot + 1) * ROWS]
            part_ref[slot, i] = pltpu.roll(both, lefts[slot], 1)[:, :WIN]

    def crop_rows(u):
        for slot in range(4):
            offset = oy_ref[slots[slot]]
            skip, rest = offset // ROWS, ROWS - offset % ROWS
            upper = iota2((2 * ROWS, WIN))[0] % ROWS < rest
            after = jnp.minimum(u + skip + 1, tiles - 1)
            value = jnp.where(upper, part_ref[slot, u + skip], part_ref[slot, after])
            ref = (slot0_ref, slot1_ref, slot2_ref, slot3_ref)[slot]
            for plane in range(2):
                rows = slice(u * ROWS, (u + 1) * ROWS)
                ref[plane, rows] = value[plane * ROWS : (plane + 1) * ROWS]

    for low, high in zip((0, *STAGES), STAGES):
        for copy in large[low:high]:
            copy.wait()
        for i in range(tiles):
            part = multiply(i, low, high)
            full_ref[i] = full_ref[i] + part if low else part
            if high == len(large):
                crop_columns(i)
                if i >= 2:
                    crop_rows(i - 2)
    crop_rows(tiles - 2)


def own_waves(s_flat, offsets_y, offsets_x, beams):
    depth = s_flat.shape[0]
    small = (offsets_y, offsets_x, *beams)
    operands = (*small, s_flat)
    return pl.pallas_call(
        waves_kernel,
        in_specs=[pl.BlockSpec(memory_space=pl.ANY)] * len(operands),
        out_specs=[pl.BlockSpec(memory_space=pltpu.VMEM)] * 4,
        out_shape=[pltpu.VMEM((2, WIN, WIN), jnp.float32)] * 4,
        scratch_shapes=[
            pltpu.SMEM(offsets_y.shape, jnp.int32),
            pltpu.SMEM(offsets_x.shape, jnp.int32),
            *[pltpu.VMEM(array.shape, array.dtype) for array in beams],
            pltpu.VMEM(s_flat.shape, s_flat.dtype),
            pltpu.VMEM((8 * ROWS, depth * ROWS), jnp.bfloat16),
            pltpu.VMEM((FIELD_Y // ROWS, 8 * ROWS, FIELD_X), jnp.float32),
            pltpu.VMEM((4, FIELD_Y // ROWS, 2 * ROWS, WIN), jnp.float32),
            pltpu.SemaphoreType.DMA((len(small),)),
            pltpu.SemaphoreType.DMA((depth // PIECE,)),
        ],
        compiler_params=pltpu.CompilerParams(vmem_limit_bytes=WHOLE),
    )(*operands)


def split(value):
    high = value.astype(jnp.bfloat16)
    return high, (value - high.astype(jnp.float32)).astype(jnp.bfloat16)


def product(left, right):
    rows, columns = left[0].shape[0], right[0].shape[1]
    if rows < columns:
        both = dot(jnp.concatenate(left, axis=0), right[0])
        return both[:rows] + (both[rows:] + dot(left[0], right[1]))
    both = dot(left[0], jnp.concatenate(right, axis=1))
    return both[:, :columns] + (both[:, columns:] + dot(left[1], right[0]))


def misfit_kernel(oy_ref, wave_ref, measured_ref, table_ref, out_ref, field_ref):
    forward = (table_ref[0, 0], table_ref[0, 1])
    inverse = (table_ref[1, 0], table_ref[1, 1])

    def side(value):
        return jnp.concatenate([value[:WIN], value[WIN:]], axis=1)

    def stack(value):
        return jnp.concatenate([value[:, :WIN], value[:, WIN:]], axis=0)

    wave = jnp.concatenate([wave_ref[0], wave_ref[1]], axis=1)
    far = product(inverse, split(stack(product(split(wave), forward))))
    far_real, far_imag = far[:WIN], far[WIN:]
    modulus = jnp.sqrt(far_real * far_real + far_imag * far_imag)
    factor = 1.0 - measured_ref[lax.rem(slot_position(0), 4)] / jnp.maximum(modulus, 0.5)
    resid = jnp.concatenate([far_real * factor, far_imag * factor], axis=0)
    back = product(split(side(product(forward, split(resid)))), inverse)
    back = jnp.concatenate([back, jnp.zeros((FIELD_Y - WIN, 2 * WIN), jnp.float32)], axis=0)
    back = pltpu.roll(back, oy_ref[slot_position(0)], 0)
    for plane in range(2):
        field_ref[plane] = back[:, plane * WIN : (plane + 1) * WIN]
    copies = out_ref.shape[1]
    zeros = jnp.zeros((BLOCK - 2 * BAND, WIN), jnp.float32)
    for band in range(BANDS):
        rows = slice(band * BAND, (band + 1) * BAND)
        block = jnp.concatenate([field_ref[0, rows], field_ref[1, rows], zeros], axis=0)
        for copy in range(copies):
            out_ref[band, copy] = block


def misfit_blocks(offsets_y, wave, measured, tables, copies):
    return pl.pallas_call(
        misfit_kernel,
        in_specs=[pl.BlockSpec(memory_space=pltpu.SMEM)] + [pl.BlockSpec(memory_space=pltpu.VMEM)] * 3,
        out_specs=pl.BlockSpec(memory_space=pltpu.VMEM),
        scratch_shapes=[pltpu.VMEM((2, FIELD_Y, WIN), jnp.float32)],
        out_shape=jax.ShapeDtypeStruct((BANDS, copies, BLOCK, WIN), jnp.float32),
        compiler_params=pltpu.CompilerParams(vmem_limit_bytes=LIMIT),
    )(offsets_y, wave, measured, tables)


TILE = 8
FULL = BAND // TILE
REST = BAND - FULL * TILE
HALF = 16
LINES = 2 * FIELD_X // WIN


def side_position(side, n):
    core = lax.axis_index("core") ^ side
    return n // 2 * 4 + 2 * core + n % 2


def spread_weights(coefs, size, row_parts, shape):
    count, beams = coefs[0].shape
    beam, plane, _ = row_parts((shape[0], beams))
    pick = one_hot(beam == iota2((shape[0], beams))[1])
    real, imag = [
        lax.dot_general(pick, coef, (((1,), (1,)), ((), ())), preferred_element_type=jnp.float32)
        for coef in coefs
    ]
    first = row_parts((shape[0], count))[1] == 0
    source, column = iota2((count, shape[1]))
    same = source == column // (2 * size)
    low = column % (2 * size) < size
    spread = dot(jnp.where(first, real, -imag).astype(jnp.bfloat16), one_hot(same & low))
    spread += dot(jnp.where(first, imag, real).astype(jnp.bfloat16), one_hot(same & ~low))
    equal = row_parts(shape)[2] == iota2(shape)[1] % size
    return jnp.where(equal, spread, 0.0).astype(jnp.bfloat16)


def weights_kernel(oy_ref, ox_ref, index_ref, amplitude_ref, phase_ref, full_ref, rest_ref):
    beams, count = index_ref.shape[1], 2 * HALF
    where = [side_position(n // HALF, n % HALF) for n in range(count)]
    shape = (count, beams)
    rows_y = places(count, lambda n: oy_ref[where[n]], shape)
    cols_x = places(count, lambda n: ox_ref[where[n]], shape)
    waves = [index_ref[0:1], index_ref[1:2], amplitude_ref[...], phase_ref[...]]
    coefs = [value.astype(jnp.bfloat16) for value in beam_weights(rows_y, cols_x, waves)]

    def full_parts(shape):
        row = iota2(shape)[0]
        return row // (2 * TILE), row // TILE % 2, row % TILE

    def rest_parts(shape):
        row = iota2(shape)[0]
        return row % beams, row // (beams * REST), row // beams % REST

    full_ref[...] = spread_weights(coefs, TILE, full_parts, full_ref.shape)
    rest_ref[...] = spread_weights(coefs, REST, rest_parts, rest_ref.shape)


def fold_weights(offsets_y, offsets_x, beams):
    rows, columns = 2 * beams[1].shape[1], 4 * HALF
    shapes = [(rows * size, columns * size) for size in (TILE, REST)]
    return pl.pallas_call(
        weights_kernel,
        in_specs=[pl.BlockSpec(memory_space=pltpu.SMEM)] * 2 + [pl.BlockSpec(memory_space=pltpu.VMEM)] * 3,
        out_specs=[pl.BlockSpec(memory_space=pltpu.VMEM)] * 2,
        out_shape=[jax.ShapeDtypeStruct(shape, jnp.bfloat16) for shape in shapes],
        compiler_params=pltpu.CompilerParams(vmem_limit_bytes=LIMIT),
        cost_estimate=pl.CostEstimate(flops=100000000, bytes_accessed=1000000, transcendentals=0),
    )(offsets_y, offsets_x, *beams)


PLACED = [(FULL, 2 * HALF * TILE, FIELD_X), (2 * HALF * REST, FIELD_X)]


def place(side, ox_ref, received_ref, full_ref, rest_ref):
    blank = jnp.zeros((2 * BAND, FIELD_X - WIN), jnp.float32)
    tails = []
    for n in range(HALF):
        shift = ox_ref[side_position(side, n)]
        both = jnp.concatenate([received_ref[n, : 2 * BAND, :], blank], axis=1)
        both = pltpu.roll(both, shift, 1)
        planes = [both[:BAND], both[BAND:]]
        for t in range(FULL):
            rows = slice(t * TILE, (t + 1) * TILE)
            pair = jnp.concatenate([planes[0][rows], planes[1][rows]], axis=0)
            full_ref[t, n * 2 * TILE : (n + 1) * 2 * TILE, :] = pair.astype(jnp.bfloat16)
        tails += [plane[FULL * TILE :] for plane in planes]
    rest_ref[...] = jnp.concatenate(tails, axis=0).astype(jnp.bfloat16)


def place_kernel(ox_ref, received_ref, full_ref, rest_ref):
    place(0, ox_ref, received_ref, full_ref, rest_ref)


def place_own(offsets_x, received):
    return pl.pallas_call(
        place_kernel,
        in_specs=[pl.BlockSpec(memory_space=pltpu.SMEM), pl.BlockSpec(memory_space=pltpu.VMEM)],
        out_specs=[pl.BlockSpec(memory_space=pltpu.VMEM)] * 2,
        out_shape=[jax.ShapeDtypeStruct(shape, jnp.bfloat16) for shape in PLACED],
        compiler_params=pltpu.CompilerParams(vmem_limit_bytes=LIMIT),
        cost_estimate=pl.CostEstimate(flops=1000000, bytes_accessed=1000000, transcendentals=0),
    )(offsets_x, received)


CHUNKS = 4


def fold_kernel(
    ox_ref, weight_ref, weight_rest_ref, own_ref, own_rest_ref, other_ref,
    out_hbm,
    full_ref, rest_ref, line_ref, sem,
):
    place(1, ox_ref, other_ref, full_ref, rest_ref)
    beams = weight_ref.shape[0] // (2 * TILE)
    length = BAND * LINES
    columns = [slice(side * WIN, (side + 1) * WIN) for side in range(FIELD_X // WIN)]

    half = own_rest_ref.shape[0]
    part = dot(weight_rest_ref[:, :half], own_rest_ref[...])
    part += dot(weight_rest_ref[:, half:], rest_ref[...])
    for group in range(2 * REST):
        plane, y = divmod(group, REST)
        value = part[group * beams : (group + 1) * beams]
        for side, column in enumerate(columns):
            start = (FULL * TILE + y) * LINES + 2 * side + plane
            line_ref[pl.ds(start, beams, stride=length), :] = value[:, column]

    half = own_ref.shape[1]
    rows, lines = weight_ref.shape[0] // CHUNKS, beams * length // CHUNKS
    copies = []
    for chunk in range(CHUNKS):
        for t in range(FULL):
            at = slice(chunk * rows, (chunk + 1) * rows)
            part = dot(weight_ref[at, :half], own_ref[t]) + dot(weight_ref[at, half:], full_ref[t])
            for group in range(rows // TILE):
                beam, plane = divmod(group, 2)
                value = part[group * TILE : (group + 1) * TILE]
                for side, column in enumerate(columns):
                    start = chunk * lines + beam * length + t * TILE * LINES + 2 * side + plane
                    line_ref[pl.ds(start, TILE, stride=LINES), :] = value[:, column]
        at = pl.ds(chunk * lines, lines)
        copy = pltpu.make_async_copy(line_ref.at[at], out_hbm.at[at], sem.at[chunk])
        copy.start()
        copies.append(copy)
    for copy in copies:
        copy.wait()


def fold(offsets_x, weights, own, other):
    lines = weights[0].shape[0] // (2 * TILE) * BAND * LINES
    operands = (*weights, *own, other)
    return pl.pallas_call(
        fold_kernel,
        in_specs=[pl.BlockSpec(memory_space=pltpu.SMEM)] + [pl.BlockSpec(memory_space=pltpu.VMEM)] * len(operands),
        out_specs=pl.BlockSpec(memory_space=pl.ANY),
        out_shape=jax.ShapeDtypeStruct((lines, WIN), jnp.float32),
        scratch_shapes=[
            *[pltpu.VMEM(shape, jnp.bfloat16) for shape in PLACED],
            pltpu.VMEM((lines + BAND * LINES, WIN), jnp.float32),
            pltpu.SemaphoreType.DMA((CHUNKS,)),
        ],
        compiler_params=pltpu.CompilerParams(vmem_limit_bytes=LIMIT),
    )(offsets_x, *operands)


def swap(value, axis, pairs):
    both = [(a, b) for a, b in pairs] + [(b, a) for a, b in pairs]
    return lax.ppermute(value, axis, both)


def body(s_matrix, beam_index, amplitude, phase, offsets_y, offsets_x, measured):
    beams_here = s_matrix.shape[0]
    depth = lax.axis_size("z")
    beams = (beam_index.T, amplitude[None, :], phase[None, :])
    s_flat = s_matrix.reshape(beams_here * 2, FIELD_Y, FIELD_X)

    slots = own_waves(s_flat, offsets_y, offsets_x, beams)
    onward = slots[1] + swap(slots[3], "core", [(0, 1)])
    total = slots[0] + swap(slots[2], "core", [(0, 1)])
    total = total + swap(onward, "yl", [(0, 1)])
    weights = fold_weights(offsets_y, offsets_x, beams)
    for bit in (1, 2):
        other = swap(total, "z", [(i, i ^ bit) for i in range(depth) if not i & bit])
        if bit == 1:
            other, weights = lax.optimization_barrier((other, weights))
        total = total + other
    total = total + swap(total, "z", [(i, depth - 1 - i) for i in range(depth // 2)])

    copies = lax.axis_size("yl")
    blocks = misfit_blocks(offsets_y, total, measured, jnp.asarray(transform_tables()), copies)
    blocks = blocks.reshape(BANDS * copies, BLOCK, WIN)
    received = lax.all_to_all(blocks, ("pos", "yl"), 0, 0, tiled=True)
    other = swap(received, "core", [(0, 1)])
    own = place_own(offsets_x, received)
    lines = fold(offsets_x, weights, own, other)
    gradient = lines.reshape(beams_here, BAND, FIELD_X // WIN, 2, WIN).transpose(0, 3, 1, 2, 4)
    return gradient.reshape(beams_here, 2, BAND, FIELD_X)


def solution(mesh):
    fine = Mesh(mesh.devices.reshape(8, 8, 2, 2), ("pos", "z", "yl", "core"))
    beam = ("z", "yl", "core")
    return jax.shard_map(
        body,
        mesh=fine,
        in_specs=(
            P(beam, None, None, None),
            P(beam, None),
            P(beam),
            P(beam),
            P(),
            P(),
            P("pos", None, None),
        ),
        out_specs=P(beam, None, "pos", None),
        check_vma=False,
    )
```

```python
import math

import jax
import jax.numpy as jnp
import numpy as np
from jax import lax
from jax.experimental import pallas as pl
from jax.experimental.pallas import tpu as pltpu
from jax.sharding import Mesh
from jax.sharding import PartitionSpec as P

WIN = 128
FIELD_Y = 144
FIELD_X = 256
BANDS = 8
BAND = FIELD_Y // BANDS
BLOCK = 40
ROWS = 16
LIMIT = 48 * 1024 * 1024
WHOLE = 60 * 1024 * 1024


def beam_weights(rows_y, cols_x, beams):
    wave_y, wave_x, amplitude, phase = beams
    cells = FIELD_Y * FIELD_X
    count = rows_y * wave_y * FIELD_X + cols_x * wave_x * FIELD_Y
    whole = jnp.floor(count.astype(jnp.float32) * (1.0 / cells)).astype(jnp.int32)
    turns = count - whole * cells
    turns = jnp.where(turns < 0, turns + cells, turns)
    turns = jnp.where(turns >= cells, turns - cells, turns)
    angles = phase - 2.0 * math.pi / cells * turns.astype(jnp.float32)
    return amplitude * jnp.cos(angles), amplitude * jnp.sin(angles)


def places(count, offset_of, shape):
    row = lax.broadcasted_iota(jnp.int32, shape, 0)
    value = jnp.zeros(shape, jnp.int32)
    for n in range(count):
        value = jnp.where(row == n, offset_of(n), value)
    return value


def one_hot(condition):
    return jnp.where(condition, 1.0, 0.0).astype(jnp.bfloat16)


def iota2(shape):
    return [lax.broadcasted_iota(jnp.int32, shape, axis) for axis in range(2)]


def dot(left, right):
    return jnp.dot(left, right, preferred_element_type=jnp.float32)


def transform_tables():
    counter = np.arange(WIN)
    angles = 2.0 * np.pi / WIN * np.mod(counter[:, None] * counter[None, :], WIN)
    cos_table, sin_table = np.cos(angles) / math.sqrt(WIN), np.sin(angles) / math.sqrt(WIN)
    table = np.block([[cos_table, -sin_table], [sin_table, cos_table]]).astype(np.float32)
    pair = np.stack([table, table.T])
    high = pair.astype(jnp.bfloat16)
    low = (pair - high.astype(np.float32)).astype(jnp.bfloat16)
    return np.stack([high, low], axis=1)


def slot_position(slot):
    core = lax.axis_index("core") ^ (slot // 2)
    lane = lax.axis_index("yl") ^ (slot % 2)
    return lax.axis_index("pos") * 4 + 2 * core + lane


PIECE = 16
STAGES = (3, 6, 8)


def waves_kernel(
    oy_hbm, ox_hbm, index_hbm, amplitude_hbm, phase_hbm, s_hbm,
    slot0_ref, slot1_ref, slot2_ref, slot3_ref,
    oy_ref, ox_ref, index_ref, amplitude_ref, phase_ref, s_ref, mix_ref, full_ref, part_ref, small_sem, piece_sem,
):
    depth, tiles = s_ref.shape[0], FIELD_Y // ROWS
    beams = depth // 2
    small = [
        pltpu.make_async_copy(source, target, small_sem.at[i])
        for i, (source, target) in enumerate(
            [
                (oy_hbm, oy_ref),
                (ox_hbm, ox_ref),
                (index_hbm, index_ref),
                (amplitude_hbm, amplitude_ref),
                (phase_hbm, phase_ref),
            ]
        )
    ]
    large = []
    for i in range(depth // PIECE):
        planes = pl.ds(i * PIECE, PIECE)
        large.append(pltpu.make_async_copy(s_hbm.at[planes], s_ref.at[planes], piece_sem.at[i]))
    for copy in small + large[: STAGES[0]]:
        copy.start()
    for copy in large[STAGES[0] :]:
        copy.start(priority=1)

    outs, wide = 8, depth * ROWS
    source, column = iota2((beams, wide))
    same = source == column // (2 * ROWS)
    first = column % (2 * ROWS) < ROWS
    picks = [one_hot(same & first), one_hot(same & ~first)]
    for copy in small:
        copy.wait()
    slots = [slot_position(slot) for slot in range(4)]
    shape = (outs, beams)
    rows_y = places(outs, lambda n: oy_ref[slots[n // 2]], shape)
    cols_x = places(outs, lambda n: ox_ref[slots[n // 2]], shape)
    waves = [index_ref[0:1], index_ref[1:2], amplitude_ref[...], phase_ref[...]]
    real, imag = beam_weights(rows_y, cols_x, waves)
    is_real = iota2(shape)[0] % 2 == 0
    spread = jnp.zeros((outs * ROWS, wide), jnp.float32)
    for coef, pick in zip(
        (jnp.where(is_real, real, imag), jnp.where(is_real, -imag, real)), picks, strict=True
    ):
        tall = jnp.broadcast_to(coef[:, None, :], (outs, ROWS, beams)).reshape(outs * ROWS, beams)
        spread += dot(tall.astype(jnp.bfloat16), pick)
    row = lax.broadcasted_iota(jnp.int32, (outs * ROWS, 1), 0)
    moved = row
    for slot in range(4):
        moved += jnp.where(row // (2 * ROWS) == slot, oy_ref[slots[slot]], 0)
    column = iota2((outs * ROWS, wide))[1]
    mix_ref[...] = jnp.where(moved % ROWS == column % ROWS, spread, 0.0).astype(jnp.bfloat16)

    lefts = [lax.rem(FIELD_X - ox_ref[slots[slot]], FIELD_X) for slot in range(4)]

    def multiply(i, low, high):
        low, high = low * PIECE, high * PIECE
        tile = s_ref[low:high, i * ROWS : (i + 1) * ROWS, :].reshape((high - low) * ROWS, FIELD_X)
        return dot(mix_ref[:, low * ROWS : high * ROWS], tile)

    def crop_columns(i):
        for slot in range(4):
            both = full_ref[i, 2 * slot * ROWS : 2 * (slot + 1) * ROWS]
            part_ref[slot, i] = pltpu.roll(both, lefts[slot], 1)[:, :WIN]

    def crop_rows(u):
        for slot in range(4):
            offset = oy_ref[slots[slot]]
            skip, rest = offset // ROWS, ROWS - offset % ROWS
            upper = iota2((2 * ROWS, WIN))[0] % ROWS < rest
            after = jnp.minimum(u + skip + 1, tiles - 1)
            value = jnp.where(upper, part_ref[slot, u + skip], part_ref[slot, after])
            ref = (slot0_ref, slot1_ref, slot2_ref, slot3_ref)[slot]
            for plane in range(2):
                rows = slice(u * ROWS, (u + 1) * ROWS)
                ref[plane, rows] = value[plane * ROWS : (plane + 1) * ROWS]

    for low, high in zip((0, *STAGES), STAGES):
        for copy in large[low:high]:
            copy.wait()
        for i in range(tiles):
            part = multiply(i, low, high)
            full_ref[i] = full_ref[i] + part if low else part
            if high == len(large):
                crop_columns(i)
                if i >= 2:
                    crop_rows(i - 2)
    crop_rows(tiles - 2)


def own_waves(s_flat, offsets_y, offsets_x, beams):
    depth = s_flat.shape[0]
    small = (offsets_y, offsets_x, *beams)
    operands = (*small, s_flat)
    return pl.pallas_call(
        waves_kernel,
        in_specs=[pl.BlockSpec(memory_space=pl.ANY)] * len(operands),
        out_specs=[pl.BlockSpec(memory_space=pltpu.VMEM)] * 4,
        out_shape=[pltpu.VMEM((2, WIN, WIN), jnp.float32)] * 4,
        scratch_shapes=[
            pltpu.SMEM(offsets_y.shape, jnp.int32),
            pltpu.SMEM(offsets_x.shape, jnp.int32),
            *[pltpu.VMEM(array.shape, array.dtype) for array in beams],
            pltpu.VMEM(s_flat.shape, s_flat.dtype),
            pltpu.VMEM((8 * ROWS, depth * ROWS), jnp.bfloat16),
            pltpu.VMEM((FIELD_Y // ROWS, 8 * ROWS, FIELD_X), jnp.float32),
            pltpu.VMEM((4, FIELD_Y // ROWS, 2 * ROWS, WIN), jnp.float32),
            pltpu.SemaphoreType.DMA((len(small),)),
            pltpu.SemaphoreType.DMA((depth // PIECE,)),
        ],
        compiler_params=pltpu.CompilerParams(vmem_limit_bytes=WHOLE),
    )(*operands)


def split(value):
    high = value.astype(jnp.bfloat16)
    return high, (value - high.astype(jnp.float32)).astype(jnp.bfloat16)


def product(left, right):
    rows, columns = left[0].shape[0], right[0].shape[1]
    if rows < columns:
        both = dot(jnp.concatenate(left, axis=0), right[0])
        return both[:rows] + (both[rows:] + dot(left[0], right[1]))
    both = dot(left[0], jnp.concatenate(right, axis=1))
    return both[:, :columns] + (both[:, columns:] + dot(left[1], right[0]))


def misfit_kernel(oy_ref, wave_ref, measured_ref, table_ref, out_ref, field_ref):
    forward = (table_ref[0, 0], table_ref[0, 1])
    inverse = (table_ref[1, 0], table_ref[1, 1])

    def side(value):
        return jnp.concatenate([value[:WIN], value[WIN:]], axis=1)

    def stack(value):
        return jnp.concatenate([value[:, :WIN], value[:, WIN:]], axis=0)

    wave = jnp.concatenate([wave_ref[0], wave_ref[1]], axis=1)
    far = product(inverse, split(stack(product(split(wave), forward))))
    far_real, far_imag = far[:WIN], far[WIN:]
    modulus = jnp.sqrt(far_real * far_real + far_imag * far_imag)
    factor = 1.0 - measured_ref[...] / jnp.maximum(modulus, 0.5)
    resid = jnp.concatenate([far_real * factor, far_imag * factor], axis=0)
    back = product(split(side(product(forward, split(resid)))), inverse)
    back = jnp.concatenate([back, jnp.zeros((FIELD_Y - WIN, 2 * WIN), jnp.float32)], axis=0)
    back = pltpu.roll(back, oy_ref[slot_position(0)], 0)
    for plane in range(2):
        field_ref[plane] = back[:, plane * WIN : (plane + 1) * WIN]
    copies = out_ref.shape[1]
    zeros = jnp.zeros((BLOCK - 2 * BAND, WIN), jnp.float32)
    for band in range(BANDS):
        rows = slice(band * BAND, (band + 1) * BAND)
        block = jnp.concatenate([field_ref[0, rows], field_ref[1, rows], zeros], axis=0)
        for copy in range(copies):
            out_ref[band, copy] = block


def misfit_blocks(offsets_y, wave, measured, tables, copies):
    return pl.pallas_call(
        misfit_kernel,
        in_specs=[pl.BlockSpec(memory_space=pltpu.SMEM)] + [pl.BlockSpec(memory_space=pltpu.VMEM)] * 3,
        out_specs=pl.BlockSpec(memory_space=pltpu.VMEM),
        scratch_shapes=[pltpu.VMEM((2, FIELD_Y, WIN), jnp.float32)],
        out_shape=jax.ShapeDtypeStruct((BANDS, copies, BLOCK, WIN), jnp.float32),
        compiler_params=pltpu.CompilerParams(vmem_limit_bytes=LIMIT),
    )(offsets_y, wave, measured, tables)


TILE = 8
FULL = BAND // TILE
REST = BAND - FULL * TILE
HALF = 16
LINES = 2 * FIELD_X // WIN


def side_position(side, n):
    core = lax.axis_index("core") ^ side
    return n // 2 * 4 + 2 * core + n % 2


def spread_weights(coefs, size, row_parts, shape):
    count, beams = coefs[0].shape
    beam, plane, _ = row_parts((shape[0], beams))
    pick = one_hot(beam == iota2((shape[0], beams))[1])
    real, imag = [
        lax.dot_general(pick, coef, (((1,), (1,)), ((), ())), preferred_element_type=jnp.float32)
        for coef in coefs
    ]
    first = row_parts((shape[0], count))[1] == 0
    source, column = iota2((count, shape[1]))
    same = source == column // (2 * size)
    low = column % (2 * size) < size
    spread = dot(jnp.where(first, real, -imag).astype(jnp.bfloat16), one_hot(same & low))
    spread += dot(jnp.where(first, imag, real).astype(jnp.bfloat16), one_hot(same & ~low))
    equal = row_parts(shape)[2] == iota2(shape)[1] % size
    return jnp.where(equal, spread, 0.0).astype(jnp.bfloat16)


def weights_kernel(
    oy_ref, ox_ref, index_ref, amplitude_ref, phase_ref, measured_hbm, table_hbm,
    full_ref, rest_ref, measured_ref, table_ref,
    sem,
):
    copies = [
        pltpu.make_async_copy(measured_hbm.at[lax.rem(slot_position(0), 4)], measured_ref, sem.at[0]),
        pltpu.make_async_copy(table_hbm, table_ref, sem.at[1]),
    ]
    for copy in copies:
        copy.start()
    beams, count = index_ref.shape[1], 2 * HALF
    where = [side_position(n // HALF, n % HALF) for n in range(count)]
    shape = (count, beams)
    rows_y = places(count, lambda n: oy_ref[where[n]], shape)
    cols_x = places(count, lambda n: ox_ref[where[n]], shape)
    waves = [index_ref[0:1], index_ref[1:2], amplitude_ref[...], phase_ref[...]]
    coefs = [value.astype(jnp.bfloat16) for value in beam_weights(rows_y, cols_x, waves)]

    def full_parts(shape):
        row = iota2(shape)[0]
        return row // (2 * TILE), row // TILE % 2, row % TILE

    def rest_parts(shape):
        row = iota2(shape)[0]
        return row % beams, row // (beams * REST), row // beams % REST

    full_ref[...] = spread_weights(coefs, TILE, full_parts, full_ref.shape)
    rest_ref[...] = spread_weights(coefs, REST, rest_parts, rest_ref.shape)
    for copy in copies:
        copy.wait()


def fold_weights(offsets_y, offsets_x, beams, measured, tables):
    rows, columns = 2 * beams[1].shape[1], 4 * HALF
    shapes = [(rows * size, columns * size) for size in (TILE, REST)]
    return pl.pallas_call(
        weights_kernel,
        in_specs=[pl.BlockSpec(memory_space=pltpu.SMEM)] * 2
        + [pl.BlockSpec(memory_space=pltpu.VMEM)] * 3
        + [pl.BlockSpec(memory_space=pl.ANY)] * 2,
        out_specs=[pl.BlockSpec(memory_space=pltpu.VMEM)] * 4,
        out_shape=[
            *[pltpu.VMEM(shape, jnp.bfloat16) for shape in shapes],
            pltpu.VMEM(measured.shape[1:], measured.dtype),
            pltpu.VMEM(tables.shape, tables.dtype),
        ],
        scratch_shapes=[pltpu.SemaphoreType.DMA((2,))],
        compiler_params=pltpu.CompilerParams(vmem_limit_bytes=WHOLE),
        cost_estimate=pl.CostEstimate(flops=100000000, bytes_accessed=1000000, transcendentals=0),
    )(offsets_y, offsets_x, *beams, measured, tables)


PLACED = [(FULL, 2 * HALF * TILE, FIELD_X), (2 * HALF * REST, FIELD_X)]


def place(side, ox_ref, received_ref, full_ref, rest_ref):
    blank = jnp.zeros((2 * BAND, FIELD_X - WIN), jnp.float32)
    tails = []
    for n in range(HALF):
        shift = ox_ref[side_position(side, n)]
        both = jnp.concatenate([received_ref[n, : 2 * BAND, :], blank], axis=1)
        both = pltpu.roll(both, shift, 1)
        planes = [both[:BAND], both[BAND:]]
        for t in range(FULL):
            rows = slice(t * TILE, (t + 1) * TILE)
            pair = jnp.concatenate([planes[0][rows], planes[1][rows]], axis=0)
            full_ref[t, n * 2 * TILE : (n + 1) * 2 * TILE, :] = pair.astype(jnp.bfloat16)
        tails += [plane[FULL * TILE :] for plane in planes]
    rest_ref[...] = jnp.concatenate(tails, axis=0).astype(jnp.bfloat16)


def place_kernel(ox_ref, received_ref, full_ref, rest_ref):
    place(0, ox_ref, received_ref, full_ref, rest_ref)


def place_own(offsets_x, received):
    return pl.pallas_call(
        place_kernel,
        in_specs=[pl.BlockSpec(memory_space=pltpu.SMEM), pl.BlockSpec(memory_space=pltpu.VMEM)],
        out_specs=[pl.BlockSpec(memory_space=pltpu.VMEM)] * 2,
        out_shape=[jax.ShapeDtypeStruct(shape, jnp.bfloat16) for shape in PLACED],
        compiler_params=pltpu.CompilerParams(vmem_limit_bytes=LIMIT),
        cost_estimate=pl.CostEstimate(flops=1000000, bytes_accessed=1000000, transcendentals=0),
    )(offsets_x, received)


CHUNKS = 4


def fold_kernel(
    ox_ref, weight_ref, weight_rest_ref, own_ref, own_rest_ref, other_ref,
    out_hbm,
    full_ref, rest_ref, line_ref, sem,
):
    place(1, ox_ref, other_ref, full_ref, rest_ref)
    beams = weight_ref.shape[0] // (2 * TILE)
    length = BAND * LINES
    columns = [slice(side * WIN, (side + 1) * WIN) for side in range(FIELD_X // WIN)]

    half = own_rest_ref.shape[0]
    part = dot(weight_rest_ref[:, :half], own_rest_ref[...])
    part += dot(weight_rest_ref[:, half:], rest_ref[...])
    for group in range(2 * REST):
        plane, y = divmod(group, REST)
        value = part[group * beams : (group + 1) * beams]
        for side, column in enumerate(columns):
            start = (FULL * TILE + y) * LINES + 2 * side + plane
            line_ref[pl.ds(start, beams, stride=length), :] = value[:, column]

    half = own_ref.shape[1]
    rows, lines = weight_ref.shape[0] // CHUNKS, beams * length // CHUNKS
    copies = []
    for chunk in range(CHUNKS):
        for t in range(FULL):
            at = slice(chunk * rows, (chunk + 1) * rows)
            part = dot(weight_ref[at, :half], own_ref[t]) + dot(weight_ref[at, half:], full_ref[t])
            for group in range(rows // TILE):
                beam, plane = divmod(group, 2)
                value = part[group * TILE : (group + 1) * TILE]
                for side, column in enumerate(columns):
                    start = chunk * lines + beam * length + t * TILE * LINES + 2 * side + plane
                    line_ref[pl.ds(start, TILE, stride=LINES), :] = value[:, column]
        at = pl.ds(chunk * lines, lines)
        copy = pltpu.make_async_copy(line_ref.at[at], out_hbm.at[at], sem.at[chunk])
        copy.start()
        copies.append(copy)
    for copy in copies:
        copy.wait()


def fold(offsets_x, weights, own, other):
    lines = weights[0].shape[0] // (2 * TILE) * BAND * LINES
    operands = (*weights, *own, other)
    return pl.pallas_call(
        fold_kernel,
        in_specs=[pl.BlockSpec(memory_space=pltpu.SMEM)] + [pl.BlockSpec(memory_space=pltpu.VMEM)] * len(operands),
        out_specs=pl.BlockSpec(memory_space=pl.ANY),
        out_shape=jax.ShapeDtypeStruct((lines, WIN), jnp.float32),
        scratch_shapes=[
            *[pltpu.VMEM(shape, jnp.bfloat16) for shape in PLACED],
            pltpu.VMEM((lines + BAND * LINES, WIN), jnp.float32),
            pltpu.SemaphoreType.DMA((CHUNKS,)),
        ],
        compiler_params=pltpu.CompilerParams(vmem_limit_bytes=LIMIT),
    )(offsets_x, *operands)


def swap(value, axis, pairs):
    both = [(a, b) for a, b in pairs] + [(b, a) for a, b in pairs]
    return lax.ppermute(value, axis, both)


def body(s_matrix, beam_index, amplitude, phase, offsets_y, offsets_x, measured):
    beams_here = s_matrix.shape[0]
    depth = lax.axis_size("z")
    beams = (beam_index.T, amplitude[None, :], phase[None, :])
    s_flat = s_matrix.reshape(beams_here * 2, FIELD_Y, FIELD_X)

    slots = own_waves(s_flat, offsets_y, offsets_x, beams)
    onward = slots[1] + swap(slots[3], "core", [(0, 1)])
    total = slots[0] + swap(slots[2], "core", [(0, 1)])
    total = total + swap(onward, "yl", [(0, 1)])
    tables = jnp.asarray(transform_tables())
    fetched = fold_weights(offsets_y, offsets_x, beams, measured, tables)
    for bit in (1, 2):
        other = swap(total, "z", [(i, i ^ bit) for i in range(depth) if not i & bit])
        if bit == 1:
            other, fetched = lax.optimization_barrier((other, fetched))
        total = total + other
    total = total + swap(total, "z", [(i, depth - 1 - i) for i in range(depth // 2)])

    *weights, own_measured, tables = fetched
    copies = lax.axis_size("yl")
    blocks = misfit_blocks(offsets_y, total, own_measured, tables, copies)
    blocks = blocks.reshape(BANDS * copies, BLOCK, WIN)
    received = lax.all_to_all(blocks, ("pos", "yl"), 0, 0, tiled=True)
    other = swap(received, "core", [(0, 1)])
    own = place_own(offsets_x, received)
    lines = fold(offsets_x, weights, own, other)
    gradient = lines.reshape(beams_here, BAND, FIELD_X // WIN, 2, WIN).transpose(0, 3, 1, 2, 4)
    return gradient.reshape(beams_here, 2, BAND, FIELD_X)


def solution(mesh):
    fine = Mesh(mesh.devices.reshape(8, 8, 2, 2), ("pos", "z", "yl", "core"))
    beam = ("z", "yl", "core")
    return jax.shard_map(
        body,
        mesh=fine,
        in_specs=(
            P(beam, None, None, None),
            P(beam, None),
            P(beam),
            P(beam),
            P(),
            P(),
            P("pos", None, None),
        ),
        out_specs=P(beam, None, "pos", None),
        check_vma=False,
    )
```

```python
import math

import jax
import jax.numpy as jnp
import numpy as np
from jax import lax
from jax.experimental import pallas as pl
from jax.experimental.pallas import tpu as pltpu
from jax.sharding import Mesh
from jax.sharding import PartitionSpec as P

WIN = 128
FIELD_Y = 144
FIELD_X = 256
BANDS = 8
BAND = FIELD_Y // BANDS
BLOCK = 40
ROWS = 16
LIMIT = 48 * 1024 * 1024
WHOLE = 60 * 1024 * 1024


def beam_weights(rows_y, cols_x, beams):
    wave_y, wave_x, amplitude, phase = beams
    cells = FIELD_Y * FIELD_X
    count = rows_y * wave_y * FIELD_X + cols_x * wave_x * FIELD_Y
    whole = jnp.floor(count.astype(jnp.float32) * (1.0 / cells)).astype(jnp.int32)
    turns = count - whole * cells
    turns = jnp.where(turns < 0, turns + cells, turns)
    turns = jnp.where(turns >= cells, turns - cells, turns)
    angles = phase - 2.0 * math.pi / cells * turns.astype(jnp.float32)
    return amplitude * jnp.cos(angles), amplitude * jnp.sin(angles)


def places(count, offset_of, shape):
    row = lax.broadcasted_iota(jnp.int32, shape, 0)
    value = jnp.zeros(shape, jnp.int32)
    for n in range(count):
        value = jnp.where(row == n, offset_of(n), value)
    return value


def one_hot(condition):
    return jnp.where(condition, 1.0, 0.0).astype(jnp.bfloat16)


def iota2(shape):
    return [lax.broadcasted_iota(jnp.int32, shape, axis) for axis in range(2)]


def dot(left, right):
    return jnp.dot(left, right, preferred_element_type=jnp.float32)


def transform_tables():
    counter = np.arange(WIN)
    angles = 2.0 * np.pi / WIN * np.mod(counter[:, None] * counter[None, :], WIN)
    cos_table, sin_table = np.cos(angles) / math.sqrt(WIN), np.sin(angles) / math.sqrt(WIN)
    table = np.block([[cos_table, -sin_table], [sin_table, cos_table]]).astype(np.float32)
    pair = np.stack([table, table.T])
    high = pair.astype(jnp.bfloat16)
    low = (pair - high.astype(np.float32)).astype(jnp.bfloat16)
    return np.stack([high, low], axis=1)


def slot_position(slot):
    core = lax.axis_index("core") ^ (slot // 2)
    lane = lax.axis_index("yl") ^ (slot % 2)
    return lax.axis_index("pos") * 4 + 2 * core + lane


PIECE = 16
STAGES = (3, 6, 8)


def waves_kernel(
    oy_hbm, ox_hbm, index_hbm, amplitude_hbm, phase_hbm, s_hbm,
    slot0_ref, slot1_ref, slot2_ref, slot3_ref,
    oy_ref, ox_ref, index_ref, amplitude_ref, phase_ref, s_ref, mix_ref, full_ref, part_ref, small_sem, piece_sem,
):
    depth, tiles = s_ref.shape[0], FIELD_Y // ROWS
    beams = depth // 2
    small = [
        pltpu.make_async_copy(source, target, small_sem.at[i])
        for i, (source, target) in enumerate(
            [
                (oy_hbm, oy_ref),
                (ox_hbm, ox_ref),
                (index_hbm, index_ref),
                (amplitude_hbm, amplitude_ref),
                (phase_hbm, phase_ref),
            ]
        )
    ]
    large = []
    for i in range(depth // PIECE):
        planes = pl.ds(i * PIECE, PIECE)
        large.append(pltpu.make_async_copy(s_hbm.at[planes], s_ref.at[planes], piece_sem.at[i]))
    for copy in small + large[: STAGES[0]]:
        copy.start()
    for copy in large[STAGES[0] :]:
        copy.start(priority=1)

    outs, wide = 8, depth * ROWS
    source, column = iota2((beams, wide))
    same = source == column // (2 * ROWS)
    first = column % (2 * ROWS) < ROWS
    picks = [one_hot(same & first), one_hot(same & ~first)]
    for copy in small:
        copy.wait()
    slots = [slot_position(slot) for slot in range(4)]
    shape = (outs, beams)
    rows_y = places(outs, lambda n: oy_ref[slots[n // 2]], shape)
    cols_x = places(outs, lambda n: ox_ref[slots[n // 2]], shape)
    waves = [index_ref[0:1], index_ref[1:2], amplitude_ref[...], phase_ref[...]]
    real, imag = beam_weights(rows_y, cols_x, waves)
    is_real = iota2(shape)[0] % 2 == 0
    spread = jnp.zeros((outs * ROWS, wide), jnp.float32)
    for coef, pick in zip(
        (jnp.where(is_real, real, imag), jnp.where(is_real, -imag, real)), picks, strict=True
    ):
        tall = jnp.broadcast_to(coef[:, None, :], (outs, ROWS, beams)).reshape(outs * ROWS, beams)
        spread += dot(tall.astype(jnp.bfloat16), pick)
    row = lax.broadcasted_iota(jnp.int32, (outs * ROWS, 1), 0)
    moved = row
    for slot in range(4):
        moved += jnp.where(row // (2 * ROWS) == slot, oy_ref[slots[slot]], 0)
    column = iota2((outs * ROWS, wide))[1]
    mix_ref[...] = jnp.where(moved % ROWS == column % ROWS, spread, 0.0).astype(jnp.bfloat16)

    lefts = [lax.rem(FIELD_X - ox_ref[slots[slot]], FIELD_X) for slot in range(4)]

    def multiply(i, low, high):
        low, high = low * PIECE, high * PIECE
        tile = s_ref[low:high, i * ROWS : (i + 1) * ROWS, :].reshape((high - low) * ROWS, FIELD_X)
        return dot(mix_ref[:, low * ROWS : high * ROWS], tile)

    def crop_columns(i):
        for slot in range(4):
            both = full_ref[i, 2 * slot * ROWS : 2 * (slot + 1) * ROWS]
            part_ref[slot, i] = pltpu.roll(both, lefts[slot], 1)[:, :WIN]

    def crop_rows(u):
        for slot in range(4):
            offset = oy_ref[slots[slot]]
            skip, rest = offset // ROWS, ROWS - offset % ROWS
            upper = iota2((2 * ROWS, WIN))[0] % ROWS < rest
            after = jnp.minimum(u + skip + 1, tiles - 1)
            value = jnp.where(upper, part_ref[slot, u + skip], part_ref[slot, after])
            ref = (slot0_ref, slot1_ref, slot2_ref, slot3_ref)[slot]
            for plane in range(2):
                rows = slice(u * ROWS, (u + 1) * ROWS)
                ref[plane, rows] = value[plane * ROWS : (plane + 1) * ROWS]

    for low, high in zip((0, *STAGES), STAGES):
        for copy in large[low:high]:
            copy.wait()
        for i in range(tiles):
            part = multiply(i, low, high)
            full_ref[i] = full_ref[i] + part if low else part
            if high == len(large):
                crop_columns(i)
                if i >= 2:
                    crop_rows(i - 2)
    crop_rows(tiles - 2)


def own_waves(s_flat, offsets_y, offsets_x, beams):
    depth = s_flat.shape[0]
    small = (offsets_y, offsets_x, *beams)
    operands = (*small, s_flat)
    return pl.pallas_call(
        waves_kernel,
        in_specs=[pl.BlockSpec(memory_space=pl.ANY)] * len(operands),
        out_specs=[pl.BlockSpec(memory_space=pltpu.VMEM)] * 4,
        out_shape=[pltpu.VMEM((2, WIN, WIN), jnp.float32)] * 4,
        scratch_shapes=[
            pltpu.SMEM(offsets_y.shape, jnp.int32),
            pltpu.SMEM(offsets_x.shape, jnp.int32),
            *[pltpu.VMEM(array.shape, array.dtype) for array in beams],
            pltpu.VMEM(s_flat.shape, s_flat.dtype),
            pltpu.VMEM((8 * ROWS, depth * ROWS), jnp.bfloat16),
            pltpu.VMEM((FIELD_Y // ROWS, 8 * ROWS, FIELD_X), jnp.float32),
            pltpu.VMEM((4, FIELD_Y // ROWS, 2 * ROWS, WIN), jnp.float32),
            pltpu.SemaphoreType.DMA((len(small),)),
            pltpu.SemaphoreType.DMA((depth // PIECE,)),
        ],
        compiler_params=pltpu.CompilerParams(vmem_limit_bytes=WHOLE),
    )(*operands)


def split(value):
    high = value.astype(jnp.bfloat16)
    return high, (value - high.astype(jnp.float32)).astype(jnp.bfloat16)


def product(left, right):
    rows, columns = left[0].shape[0], right[0].shape[1]
    if rows < columns:
        both = dot(jnp.concatenate(left, axis=0), right[0])
        return both[:rows] + (both[rows:] + dot(left[0], right[1]))
    both = dot(left[0], jnp.concatenate(right, axis=1))
    return both[:, :columns] + (both[:, columns:] + dot(left[1], right[0]))


def misfit_kernel(oy_ref, wave_ref, measured_ref, table_ref, out_ref, field_ref):
    forward = (table_ref[0, 0], table_ref[0, 1])
    inverse = (table_ref[1, 0], table_ref[1, 1])

    def side(value):
        return jnp.concatenate([value[:WIN], value[WIN:]], axis=1)

    def stack(value):
        return jnp.concatenate([value[:, :WIN], value[:, WIN:]], axis=0)

    wave = jnp.concatenate([wave_ref[0], wave_ref[1]], axis=1)
    far = product(inverse, split(stack(product(split(wave), forward))))
    far_real, far_imag = far[:WIN], far[WIN:]
    modulus = jnp.sqrt(far_real * far_real + far_imag * far_imag)
    factor = 1.0 - measured_ref[...] / jnp.maximum(modulus, 0.5)
    resid = jnp.concatenate([far_real * factor, far_imag * factor], axis=0)
    back = product(split(side(product(forward, split(resid)))), inverse)
    back = jnp.concatenate([back, jnp.zeros((FIELD_Y - WIN, 2 * WIN), jnp.float32)], axis=0)
    back = pltpu.roll(back, oy_ref[slot_position(0)], 0)
    for plane in range(2):
        field_ref[plane] = back[:, plane * WIN : (plane + 1) * WIN]
    copies = out_ref.shape[1]
    zeros = jnp.zeros((BLOCK - 2 * BAND, WIN), jnp.float32)
    for band in range(BANDS):
        rows = slice(band * BAND, (band + 1) * BAND)
        block = jnp.concatenate([field_ref[0, rows], field_ref[1, rows], zeros], axis=0)
        for copy in range(copies):
            out_ref[band, copy] = block


def misfit_blocks(offsets_y, wave, measured, tables, copies):
    return pl.pallas_call(
        misfit_kernel,
        in_specs=[pl.BlockSpec(memory_space=pltpu.SMEM)] + [pl.BlockSpec(memory_space=pltpu.VMEM)] * 3,
        out_specs=pl.BlockSpec(memory_space=pltpu.VMEM),
        scratch_shapes=[pltpu.VMEM((2, FIELD_Y, WIN), jnp.float32)],
        out_shape=jax.ShapeDtypeStruct((BANDS, copies, BLOCK, WIN), jnp.float32),
        compiler_params=pltpu.CompilerParams(vmem_limit_bytes=LIMIT),
    )(offsets_y, wave, measured, tables)


TILE = 8
FULL = BAND // TILE
REST = BAND - FULL * TILE
HALF = 16
LINES = 2 * FIELD_X // WIN


def side_position(side, n):
    core = lax.axis_index("core") ^ side
    return n // 2 * 4 + 2 * core + n % 2


def spread_weights(coefs, size, row_parts, shape):
    count, beams = coefs[0].shape
    beam, plane, _ = row_parts((shape[0], beams))
    pick = one_hot(beam == iota2((shape[0], beams))[1])
    real, imag = [
        lax.dot_general(pick, coef, (((1,), (1,)), ((), ())), preferred_element_type=jnp.float32)
        for coef in coefs
    ]
    first = row_parts((shape[0], count))[1] == 0
    source, column = iota2((count, shape[1]))
    same = source == column // (2 * size)
    low = column % (2 * size) < size
    spread = dot(jnp.where(first, real, -imag).astype(jnp.bfloat16), one_hot(same & low))
    spread += dot(jnp.where(first, imag, real).astype(jnp.bfloat16), one_hot(same & ~low))
    equal = row_parts(shape)[2] == iota2(shape)[1] % size
    return jnp.where(equal, spread, 0.0).astype(jnp.bfloat16)


def weights_kernel(
    oy_ref, ox_ref, index_ref, amplitude_ref, phase_ref, measured_hbm, table_hbm,
    full_ref, rest_ref, measured_ref, table_ref,
    sem,
):
    copies = [
        pltpu.make_async_copy(measured_hbm.at[lax.rem(slot_position(0), 4)], measured_ref, sem.at[0]),
        pltpu.make_async_copy(table_hbm, table_ref, sem.at[1]),
    ]
    for copy in copies:
        copy.start()
    beams, count = index_ref.shape[1], 2 * HALF
    where = [side_position(n // HALF, n % HALF) for n in range(count)]
    shape = (count, beams)
    rows_y = places(count, lambda n: oy_ref[where[n]], shape)
    cols_x = places(count, lambda n: ox_ref[where[n]], shape)
    waves = [index_ref[0:1], index_ref[1:2], amplitude_ref[...], phase_ref[...]]
    coefs = [value.astype(jnp.bfloat16) for value in beam_weights(rows_y, cols_x, waves)]

    def full_parts(shape):
        row = iota2(shape)[0]
        return row // (2 * TILE), row // TILE % 2, row % TILE

    def rest_parts(shape):
        row = iota2(shape)[0]
        return row % beams, row // (beams * REST), row // beams % REST

    full_ref[...] = spread_weights(coefs, TILE, full_parts, full_ref.shape)
    rest_ref[...] = spread_weights(coefs, REST, rest_parts, rest_ref.shape)
    for copy in copies:
        copy.wait()


def fold_weights(offsets_y, offsets_x, beams, measured, tables):
    rows, columns = 2 * beams[1].shape[1], 4 * HALF
    shapes = [(rows * size, columns * size) for size in (TILE, REST)]
    return pl.pallas_call(
        weights_kernel,
        in_specs=[pl.BlockSpec(memory_space=pltpu.SMEM)] * 2
        + [pl.BlockSpec(memory_space=pltpu.VMEM)] * 3
        + [pl.BlockSpec(memory_space=pl.ANY)] * 2,
        out_specs=[pl.BlockSpec(memory_space=pltpu.VMEM)] * 4,
        out_shape=[
            *[pltpu.VMEM(shape, jnp.bfloat16) for shape in shapes],
            pltpu.VMEM(measured.shape[1:], measured.dtype),
            pltpu.VMEM(tables.shape, tables.dtype),
        ],
        scratch_shapes=[pltpu.SemaphoreType.DMA((2,))],
        compiler_params=pltpu.CompilerParams(vmem_limit_bytes=WHOLE),
        cost_estimate=pl.CostEstimate(flops=100000000, bytes_accessed=1000000, transcendentals=0),
    )(offsets_y, offsets_x, *beams, measured, tables)


PLACED = [(FULL, 2 * HALF * TILE, FIELD_X), (2 * HALF * REST, FIELD_X)]


def place(side, ox_ref, received_ref, full_ref, rest_ref):
    blank = jnp.zeros((2 * BAND, FIELD_X - WIN), jnp.float32)
    tails = []
    for n in range(HALF):
        shift = ox_ref[side_position(side, n)]
        both = jnp.concatenate([received_ref[n, : 2 * BAND, :], blank], axis=1)
        both = pltpu.roll(both, shift, 1)
        planes = [both[:BAND], both[BAND:]]
        for t in range(FULL):
            rows = slice(t * TILE, (t + 1) * TILE)
            pair = jnp.concatenate([planes[0][rows], planes[1][rows]], axis=0)
            full_ref[t, n * 2 * TILE : (n + 1) * 2 * TILE, :] = pair.astype(jnp.bfloat16)
        tails += [plane[FULL * TILE :] for plane in planes]
    rest_ref[...] = jnp.concatenate(tails, axis=0).astype(jnp.bfloat16)


def place_kernel(ox_ref, received_ref, full_ref, rest_ref):
    place(0, ox_ref, received_ref, full_ref, rest_ref)


def place_own(offsets_x, received):
    return pl.pallas_call(
        place_kernel,
        in_specs=[pl.BlockSpec(memory_space=pltpu.SMEM), pl.BlockSpec(memory_space=pltpu.VMEM)],
        out_specs=[pl.BlockSpec(memory_space=pltpu.VMEM)] * 2,
        out_shape=[jax.ShapeDtypeStruct(shape, jnp.bfloat16) for shape in PLACED],
        compiler_params=pltpu.CompilerParams(vmem_limit_bytes=LIMIT),
        cost_estimate=pl.CostEstimate(flops=1000000, bytes_accessed=1000000, transcendentals=0),
    )(offsets_x, received)


CHUNKS = 4


def fold_kernel(
    ox_ref, weight_ref, weight_rest_ref, own_ref, own_rest_ref, other_ref,
    out_hbm,
    full_ref, rest_ref, line_ref, sem,
):
    place(1, ox_ref, other_ref, full_ref, rest_ref)
    beams = weight_ref.shape[0] // (2 * TILE)
    length = BAND * LINES
    columns = [slice(side * WIN, (side + 1) * WIN) for side in range(FIELD_X // WIN)]

    half = own_rest_ref.shape[0]
    part = dot(weight_rest_ref[:, :half], own_rest_ref[...])
    part += dot(weight_rest_ref[:, half:], rest_ref[...])
    for group in range(2 * REST):
        plane, y = divmod(group, REST)
        value = part[group * beams : (group + 1) * beams]
        for side, column in enumerate(columns):
            start = (FULL * TILE + y) * LINES + 2 * side + plane
            line_ref[pl.ds(start, beams, stride=length), :] = value[:, column]

    half = own_ref.shape[1]
    rows, lines = weight_ref.shape[0] // CHUNKS, beams * length // CHUNKS
    copies = []
    for chunk in range(CHUNKS):
        for t in range(FULL):
            at = slice(chunk * rows, (chunk + 1) * rows)
            part = dot(weight_ref[at, :half], own_ref[t]) + dot(weight_ref[at, half:], full_ref[t])
            for group in range(rows // TILE):
                beam, plane = divmod(group, 2)
                value = part[group * TILE : (group + 1) * TILE]
                for side, column in enumerate(columns):
                    start = chunk * lines + beam * length + t * TILE * LINES + 2 * side + plane
                    line_ref[pl.ds(start, TILE, stride=LINES), :] = value[:, column]
        at = pl.ds(chunk * lines, lines)
        copy = pltpu.make_async_copy(line_ref.at[at], out_hbm.at[at], sem.at[chunk])
        copy.start()
        copies.append(copy)
    for copy in copies:
        copy.wait()


def fold(offsets_x, weights, own, other):
    lines = weights[0].shape[0] // (2 * TILE) * BAND * LINES
    operands = (*weights, *own, other)
    return pl.pallas_call(
        fold_kernel,
        in_specs=[pl.BlockSpec(memory_space=pltpu.SMEM)] + [pl.BlockSpec(memory_space=pltpu.VMEM)] * len(operands),
        out_specs=pl.BlockSpec(memory_space=pl.ANY),
        out_shape=jax.ShapeDtypeStruct((lines, WIN), jnp.float32),
        scratch_shapes=[
            *[pltpu.VMEM(shape, jnp.bfloat16) for shape in PLACED],
            pltpu.VMEM((lines + BAND * LINES, WIN), jnp.float32),
            pltpu.SemaphoreType.DMA((CHUNKS,)),
        ],
        compiler_params=pltpu.CompilerParams(vmem_limit_bytes=LIMIT),
    )(offsets_x, *operands)


def swap(value, axis, pairs):
    both = [(a, b) for a, b in pairs] + [(b, a) for a, b in pairs]
    return lax.ppermute(value, axis, both)


def body(s_matrix, beam_index, amplitude, phase, offsets_y, offsets_x, measured):
    beams_here = s_matrix.shape[0]
    depth = lax.axis_size("z")
    beams = (beam_index.T, amplitude[None, :], phase[None, :])
    s_flat = s_matrix.reshape(beams_here * 2, FIELD_Y, FIELD_X)

    slots = own_waves(s_flat, offsets_y, offsets_x, beams)
    onward = slots[1] + swap(slots[3], "core", [(0, 1)])
    onward, later = lax.optimization_barrier((onward, slots[2]))
    total = slots[0] + swap(later, "core", [(0, 1)])
    total = total + swap(onward, "yl", [(0, 1)])
    tables = jnp.asarray(transform_tables())
    fetched = fold_weights(offsets_y, offsets_x, beams, measured, tables)
    for bit in (1, 2):
        other = swap(total, "z", [(i, i ^ bit) for i in range(depth) if not i & bit])
        if bit == 1:
            other, fetched = lax.optimization_barrier((other, fetched))
        total = total + other
    total = total + swap(total, "z", [(i, depth - 1 - i) for i in range(depth // 2)])

    *weights, own_measured, tables = fetched
    copies = lax.axis_size("yl")
    blocks = misfit_blocks(offsets_y, total, own_measured, tables, copies)
    blocks = blocks.reshape(BANDS * copies, BLOCK, WIN)
    received = lax.all_to_all(blocks, ("pos", "yl"), 0, 0, tiled=True)
    other = swap(received, "core", [(0, 1)])
    own = place_own(offsets_x, received)
    lines = fold(offsets_x, weights, own, other)
    gradient = lines.reshape(beams_here, BAND, FIELD_X // WIN, 2, WIN).transpose(0, 3, 1, 2, 4)
    return gradient.reshape(beams_here, 2, BAND, FIELD_X)


def solution(mesh):
    fine = Mesh(mesh.devices.reshape(8, 8, 2, 2), ("pos", "z", "yl", "core"))
    beam = ("z", "yl", "core")
    return jax.shard_map(
        body,
        mesh=fine,
        in_specs=(
            P(beam, None, None, None),
            P(beam, None),
            P(beam),
            P(beam),
            P(),
            P(),
            P("pos", None, None),
        ),
        out_specs=P(beam, None, "pos", None),
        check_vma=False,
    )
```
